32 devices in a mesh: dp: 4 (over y, core), space: 8 (over z, x).
Axes of the slice: x: 2, y: 2, z: 4, core: 2. Of those that a mesh axis runs over, the one named last changes fastest.
Arguments:
- fields: bfloat16 [4, 8, 2, 16, 64, 128], P('dp', 'space'), may hold values from -6 to 6
- conv_fine: bfloat16 [27, 128, 128], replicated, may hold values from -0.109375 to 0.109375
- conv_down: bfloat16 [1024, 256], replicated, may hold values from -0.1875 to 0.1875
- conv_depth: float32 [27, 256], replicated, may hold values from -1.5 to 1.5
- norm_gain: float32 [256], replicated, may hold values from 0.5 to 2
- conv_point: bfloat16 [256, 256], replicated, may hold values from -0.375 to 0.375
- upstream: bfloat16 [4, 8, 1, 8, 32, 256], P('dp', 'space'), may hold values from -6 to 6
Outputs:
- coarse_out: bfloat16 [4, 8, 1, 8, 32, 256], P('dp', 'space')
- grad_fine: float32 [27, 128, 128], replicated
- grad_down: float32 [1024, 256], replicated
- grad_depth_w: float32 [27, 256], replicated
- grad_gain: float32 [256], replicated
- grad_point: float32 [256, 256], replicated
The draws below stay inside these ranges and needn't reach their ends.
All inputs are finite; a program needn't handle non-finite values.
Results may differ from the reference program's by a relative error of at most 0.0081.
Values may be sent and summed in bfloat16 or wider, within the bound.
A program may use at most 128 MiB of HBM per device.

```python
import math
import jax
import jax.numpy as jnp
from jax import lax

C_FINE = 128
C_COARSE = 256
SIDE = 64
BX = 2
SAMPLES = 4
BRICKS = 8


def level_of(rng, shape, cuts, low, high):
    gain, own = 1.0, jax.random.fold_in(rng, 6)
    for axis_at, parts in cuts:
        heights = jnp.exp(jax.random.uniform(jax.random.fold_in(own, axis_at), (parts,), jnp.float32, low / len(cuts), high / len(cuts)))
        gain = gain * jnp.repeat(heights, shape[axis_at] // parts).reshape([-1 if axis == axis_at else 1 for axis in range(len(shape))])
    return gain


def centred(key, shape, deviation, reach, cuts=(), kind=jnp.bfloat16):
    level = level_of(key, shape, cuts, -0.22, 0.18) if cuts else 1.0
    array = jax.random.normal(key, shape, jnp.float32) * deviation * level
    return jnp.minimum(jnp.maximum(array, -reach), reach).astype(kind)


def setup_inputs(seed: int = 0) -> dict:
    streams_of = jax.random.split(jax.random.key(seed), 8)
    fields = centred(streams_of[0], (SAMPLES, BRICKS, BX, SIDE // 4, SIDE, C_FINE), 1.0, 6.0, ((0, 4), (1, 8)))
    conv_fine = centred(streams_of[1], (27, C_FINE, C_FINE), (27 * C_FINE) ** -0.5, 0.109375)
    conv_down = centred(streams_of[2], (8 * C_FINE, C_COARSE), (8 * C_FINE) ** -0.5, 0.1875)
    conv_depth = centred(streams_of[3], (27, C_COARSE), 0.25, 1.5, (), jnp.float32)
    norm_gain = jnp.clip(jnp.exp(jax.random.uniform(streams_of[4], (C_COARSE,), jnp.float32, math.log(0.5), math.log(2.0))), 0.5, 2.0)
    conv_point = centred(streams_of[5], (C_COARSE, C_COARSE), C_COARSE ** -0.5, 0.375)
    upstream = centred(streams_of[6], (SAMPLES, BRICKS, BX // 2, SIDE // 8, SIDE // 2, C_COARSE), 1.0, 6.0, ((0, 4), (1, 8)))
    return {"fields": fields, "conv_fine": conv_fine, "conv_down": conv_down, "conv_depth": conv_depth, "norm_gain": norm_gain, "conv_point": conv_point, "upstream": upstream}


eps = 1e-05

def tap_offsets(tap_index):
    return (tap_index // 9, tap_index // 3 % 3, tap_index % 3)

def pad_three(field):
    return jnp.pad(field, ((1, 1), (1, 1), (1, 1), (0, 0)))

def join_bricks(bricks):
    count, brick_x, brick_y, ext_z, chans = bricks.shape
    split = bricks.reshape(count // 4, 4, brick_x, brick_y, ext_z, chans)
    return split.transpose(0, 2, 1, 3, 4, 5).reshape(count // 4 * brick_x, 4 * brick_y, ext_z, chans)

def split_bricks(grid, count):
    ext_x, ext_y, ext_z, chans = grid.shape
    brick_x = ext_x // (count // 4)
    brick_y = ext_y // 4
    split = grid.reshape(count // 4, brick_x, 4, brick_y, ext_z, chans)
    return split.transpose(0, 2, 1, 3, 4, 5).reshape(count, brick_x, brick_y, ext_z, chans)

def full_conv(padded, w_taps):
    ext_x, ext_y, ext_z = (padded.shape[0] - 2, padded.shape[1] - 2, padded.shape[2] - 2)
    summed = jnp.zeros((ext_x * ext_y * ext_z, w_taps.shape[2]), jnp.float32)
    for tap_index in range(27):
        shift_x, shift_y, shift_z = tap_offsets(tap_index)
        window = padded[shift_x:shift_x + ext_x, shift_y:shift_y + ext_y, shift_z:shift_z + ext_z].reshape(-1, padded.shape[3])
        summed = summed + jnp.dot(window, w_taps[tap_index], preferred_element_type=jnp.float32)
    return summed

def tap_grads(padded, grad_rows):
    ext_x, ext_y, ext_z = (padded.shape[0] - 2, padded.shape[1] - 2, padded.shape[2] - 2)
    result = []
    for tap_index in range(27):
        shift_x, shift_y, shift_z = tap_offsets(tap_index)
        window = padded[shift_x:shift_x + ext_x, shift_y:shift_y + ext_y, shift_z:shift_z + ext_z].reshape(-1, padded.shape[3])
        result.append(lax.dot_general(window, grad_rows, (((0,), (0,)), ((), ())), preferred_element_type=jnp.float32))
    return jnp.stack(result)

def depth_conv(padded, weights):
    ext_x, ext_y, ext_z = (padded.shape[0] - 2, padded.shape[1] - 2, padded.shape[2] - 2)
    summed = jnp.zeros((ext_x, ext_y, ext_z, padded.shape[3]), jnp.float32)
    for tap_index in range(27):
        shift_x, shift_y, shift_z = tap_offsets(tap_index)
        window = padded[shift_x:shift_x + ext_x, shift_y:shift_y + ext_y, shift_z:shift_z + ext_z]
        summed = summed + window.astype(jnp.float32) * weights[tap_index]
    return summed

def depth_taps(padded, grad_field):
    ext_x, ext_y, ext_z = (padded.shape[0] - 2, padded.shape[1] - 2, padded.shape[2] - 2)
    grad_f = grad_field.astype(jnp.float32)
    result = []
    for tap_index in range(27):
        shift_x, shift_y, shift_z = tap_offsets(tap_index)
        window = padded[shift_x:shift_x + ext_x, shift_y:shift_y + ext_y, shift_z:shift_z + ext_z]
        result.append(lax.optimization_barrier(jnp.sum(window.astype(jnp.float32) * grad_f, axis=(0, 1, 2))))
    return jnp.stack(result)

def to_blocks(grid):
    ext_x, ext_y, ext_z, chans = grid.shape
    split = grid.reshape(ext_x // 2, 2, ext_y // 2, 2, ext_z // 2, 2, chans)
    return split.transpose(0, 2, 4, 1, 3, 5, 6).reshape(-1, 8 * chans)

def from_blocks(rows, ext_x, ext_y, ext_z, chans):
    split = rows.reshape(ext_x // 2, ext_y // 2, ext_z // 2, 2, 2, 2, chans)
    return split.transpose(0, 3, 1, 4, 2, 5, 6).reshape(-1, chans)

def silu_slope(value):
    sigma = jax.nn.sigmoid(value)
    return sigma * (1.0 + value * (1.0 - sigma))

def reference(fields, conv_fine, conv_down, conv_depth, norm_gain, conv_point, upstream):
    outputs = []
    brick_count = fields.shape[1]
    acc_fine = jnp.zeros(conv_fine.shape, jnp.float32)
    acc_down = jnp.zeros(conv_down.shape, jnp.float32)
    acc_depth = jnp.zeros(conv_depth.shape, jnp.float32)
    acc_gain = jnp.zeros(norm_gain.shape, jnp.float32)
    acc_point = jnp.zeros(conv_point.shape, jnp.float32)
    for sample in range(fields.shape[0]):
        fine = join_bricks(fields[sample])
        ext_x, ext_y, ext_z, chan_fine = fine.shape
        fine_pad = pad_three(fine)
        pre_act = full_conv(fine_pad, conv_fine)
        act = jax.nn.silu(pre_act).astype(jnp.bfloat16)
        blocks = to_blocks(act.reshape(ext_x, ext_y, ext_z, chan_fine))
        coarse = jnp.dot(blocks, conv_down, preferred_element_type=jnp.float32).astype(jnp.bfloat16)
        chan_coarse = coarse.shape[1]
        grid = coarse.reshape(ext_x // 2, ext_y // 2, ext_z // 2, chan_coarse)
        grid_pad = pad_three(grid)
        depth_out = depth_conv(grid_pad, conv_depth)
        count = ext_x // 2 * (ext_y // 2) * (ext_z // 2)
        scale = lax.rsqrt(lax.optimization_barrier(jnp.sum(depth_out * depth_out, axis=(0, 1, 2))) / count + eps)
        normed = (depth_out * (norm_gain * scale)).astype(jnp.bfloat16)
        normed_rows = normed.reshape(-1, chan_coarse)
        activated = jax.nn.silu(normed_rows.astype(jnp.float32)).astype(jnp.bfloat16)
        outcome = coarse.astype(jnp.float32) + jnp.dot(activated, conv_point, preferred_element_type=jnp.float32)
        outputs.append(split_bricks(outcome.astype(jnp.bfloat16).reshape(grid.shape), brick_count))
        grad_rows = join_bricks(upstream[sample]).reshape(-1, chan_coarse)
        acc_point = acc_point + lax.dot_general(activated, grad_rows, (((0,), (0,)), ((), ())), preferred_element_type=jnp.float32)
        grad_act = lax.dot_general(grad_rows, conv_point, (((1,), (1,)), ((), ())), preferred_element_type=jnp.float32)
        grad_normed = (grad_act * silu_slope(normed_rows.astype(jnp.float32))).astype(jnp.bfloat16)
        grad_f = grad_normed.reshape(grid.shape).astype(jnp.float32)
        cross = lax.optimization_barrier(jnp.sum(grad_f * depth_out, axis=(0, 1, 2)))
        acc_gain = acc_gain + scale * cross
        grad_depth_in = (norm_gain * scale * grad_f - depth_out * (norm_gain * scale * scale * scale / count) * cross).astype(jnp.bfloat16)
        acc_depth = acc_depth + depth_taps(grid_pad, grad_depth_in)
        back_depth = depth_conv(pad_three(grad_depth_in), conv_depth[::-1]).astype(jnp.bfloat16)
        grad_coarse = (grad_rows.astype(jnp.float32) + back_depth.reshape(-1, chan_coarse).astype(jnp.float32)).astype(jnp.bfloat16)
        acc_down = acc_down + lax.dot_general(blocks, grad_coarse, (((0,), (0,)), ((), ())), preferred_element_type=jnp.float32)
        grad_blocks = lax.dot_general(grad_coarse, conv_down, (((1,), (1,)), ((), ())), preferred_element_type=jnp.float32)
        grad_act_fine = from_blocks(grad_blocks, ext_x, ext_y, ext_z, chan_fine)
        grad_pre = (grad_act_fine * silu_slope(pre_act)).astype(jnp.bfloat16)
        acc_fine = acc_fine + tap_grads(fine_pad, grad_pre)
    return (jnp.stack(outputs), acc_fine, acc_down, acc_depth, acc_gain, acc_point)
```

```python
import functools
import jax
import jax.numpy as jnp
from jax import lax
from jax.experimental import pallas as pl
from jax.experimental.pallas import tpu as pltpu
from jax.sharding import PartitionSpec as P

eps = 1e-05
MESH = pl.DeviceIdType.MESH
OFFSETS = [(dx, dy) for dx in (-1, 0, 1) for dy in (-1, 0, 1) if (dx, dy) != (0, 0)]
VMEM_SPEC = pl.BlockSpec(memory_space=pltpu.VMEM)
VMEM_BYTES = 40 * 1024 * 1024


def tap_offsets(tap_index):
    return (tap_index // 9, tap_index // 3 % 3, tap_index % 3)


def full_conv(padded, w_taps):
    ext_x, ext_y, ext_z = (padded.shape[0] - 2, padded.shape[1] - 2, padded.shape[2] - 2)
    summed = jnp.zeros((ext_x * ext_y * ext_z, w_taps.shape[2]), jnp.float32)
    for tap_index in range(27):
        shift_x, shift_y, shift_z = tap_offsets(tap_index)
        window = padded[
            shift_x : shift_x + ext_x, shift_y : shift_y + ext_y, shift_z : shift_z + ext_z
        ].reshape(-1, padded.shape[3])
        summed = summed + jnp.dot(window, w_taps[tap_index], preferred_element_type=jnp.float32)
    return summed


def tap_grads(padded, grad_rows):
    ext_x, ext_y, ext_z = (padded.shape[0] - 2, padded.shape[1] - 2, padded.shape[2] - 2)
    result = []
    for tap_index in range(27):
        shift_x, shift_y, shift_z = tap_offsets(tap_index)
        window = padded[
            shift_x : shift_x + ext_x, shift_y : shift_y + ext_y, shift_z : shift_z + ext_z
        ].reshape(-1, padded.shape[3])
        result.append(
            lax.dot_general(
                window, grad_rows, (((0,), (0,)), ((), ())), preferred_element_type=jnp.float32
            )
        )
    return jnp.stack(result)


def to_blocks(grid):
    ext_x, ext_y, ext_z, chans = grid.shape
    split = grid.reshape(ext_x // 2, 2, ext_y // 2, 2, ext_z // 2, 2, chans)
    return split.transpose(0, 2, 4, 1, 3, 5, 6).reshape(-1, 8 * chans)


def from_blocks(rows, ext_x, ext_y, ext_z, chans):
    split = rows.reshape(ext_x // 2, ext_y // 2, ext_z // 2, 2, 2, 2, chans)
    return split.transpose(0, 3, 1, 4, 2, 5, 6).reshape(-1, chans)


def silu_slope(value):
    sigma = jax.nn.sigmoid(value)
    return sigma * (1.0 + value * (1.0 - sigma))


def greet_sample(nodes):
    me, dp = lax.axis_index("space"), lax.axis_index("dp")
    barrier = pltpu.get_barrier_semaphore()
    for step in range(1, nodes):
        peer = lax.rem(me + step, nodes)
        pl.semaphore_signal(barrier, inc=1, device_id=(dp, peer), device_id_type=MESH)
    pl.semaphore_wait(barrier, nodes - 1)


def edge_of(delta, ext):
    return {-1: pl.ds(0, 1), 0: pl.ds(0, ext), 1: pl.ds(ext - 1, 1)}[delta]


def rim_of(delta, ext):
    return {-1: pl.ds(0, 1), 0: pl.ds(1, ext), 1: pl.ds(ext + 1, 1)}[delta]


def halo_copies(src, dst, send_sem, recv_sem, nodes):
    me, dp = lax.axis_index("space"), lax.axis_index("dp")
    ext_x, ext_y = src.shape[0], src.shape[1]
    pos_x, pos_y = me // 4, lax.rem(me, 4)
    result = []
    for k, (dx, dy) in enumerate(OFFSETS):
        exists = jnp.logical_and(
            jnp.logical_and(pos_x + dx >= 0, pos_x + dx < nodes // 4),
            jnp.logical_and(pos_y + dy >= 0, pos_y + dy < 4),
        )
        source = src.at[edge_of(dx, ext_x), edge_of(dy, ext_y)]
        peer = (dp, me + 4 * dx + dy)
        send = pltpu.make_async_remote_copy(
            src_ref=source,
            dst_ref=dst.at[rim_of(-dx, ext_x), rim_of(-dy, ext_y)],
            send_sem=send_sem.at[k],
            recv_sem=recv_sem.at[7 - k],
            device_id=peer,
            device_id_type=MESH,
        )
        arrival = pltpu.make_async_remote_copy(
            src_ref=source,
            dst_ref=dst.at[rim_of(dx, ext_x), rim_of(dy, ext_y)],
            send_sem=send_sem.at[k],
            recv_sem=recv_sem.at[k],
            device_id=peer,
            device_id_type=MESH,
        )
        result.append((exists, send, arrival))
    return result


def start_all(copies):
    for exists, send, _ in copies:
        pl.when(exists)(send.start)


def finish_all(copies):
    for exists, _, arrival in copies:
        pl.when(exists)(arrival.wait)


def halo_kernel(nodes, src, out, send_sem, recv_sem):
    ext_x, ext_y = src.shape[0], src.shape[1]
    out[...] = jnp.zeros_like(out)
    greet_sample(nodes)
    copies = halo_copies(src, out, send_sem, recv_sem, nodes)
    start_all(copies)
    out[pl.ds(1, ext_x), pl.ds(1, ext_y)] = src[...]
    finish_all(copies)


def fine_halo(fine, nodes):
    ext_x, ext_y, ext_z, chans = fine.shape
    return pl.pallas_call(
        functools.partial(halo_kernel, nodes),
        out_shape=jax.ShapeDtypeStruct((ext_x + 2, ext_y + 2, ext_z, chans), fine.dtype),
        in_specs=[VMEM_SPEC],
        out_specs=VMEM_SPEC,
        scratch_shapes=[pltpu.SemaphoreType.DMA((8,)), pltpu.SemaphoreType.DMA((8,))],
        compiler_params=pltpu.CompilerParams(
            collective_id=0, has_side_effects=True, vmem_limit_bytes=VMEM_BYTES
        ),
        name="fine_halo",
    )(fine)


def fold8(rows):
    return jnp.sum(rows.reshape(rows.shape[0] // 8, 8, rows.shape[1]), axis=0)


def spread_copies(own, slots, send_sem, recv_sem, nodes):
    me, dp = lax.axis_index("space"), lax.axis_index("dp")
    return [
        pltpu.make_async_remote_copy(
            src_ref=own,
            dst_ref=slots.at[step],
            send_sem=send_sem.at[step],
            recv_sem=recv_sem.at[step],
            device_id=(dp, lax.rem(me + step, nodes)),
            device_id_type=MESH,
        )
        for step in range(1, nodes)
    ]


def fill_grid(grid, padded):
    ext_z = padded.shape[2]
    side = jnp.zeros(grid.shape[:2] + (8, grid.shape[3]), jnp.float32)
    grid[:, :, pl.ds(0, 8)] = side
    grid[:, :, pl.ds(8 + ext_z, 8)] = side
    grid[:, :, pl.ds(8, ext_z)] = padded[...].astype(jnp.float32)


def coarse_kernel(
    nodes, coarse, up, depth_w, gain_ref, point_w,
    out, grad_coarse, grad_point, grad_depth, grad_gain,
    c_pad, g_pad, g_own, c_grid, g_grid, depth_out, g_act,
    own_1, own_2, slots_1, slots_2,
    sem_a, sem_b, sem_c, sem_d, sem_e, sem_f, sem_g, sem_h,
):
    ext_x, ext_y, ext_z, chans = coarse.shape
    cells = ext_x * ext_y * ext_z
    count = nodes * cells
    c_pad[...] = jnp.zeros_like(c_pad)
    g_pad[...] = jnp.zeros_like(g_pad)
    greet_sample(nodes)
    first = halo_copies(coarse, c_pad, sem_a, sem_b, nodes)
    start_all(first)
    c_pad[pl.ds(1, ext_x), pl.ds(1, ext_y)] = coarse[...]
    up_rows = up[...].reshape(cells, chans)
    g_act[...] = lax.dot_general(
        up_rows, point_w[...], (((1,), (1,)), ((), ())), preferred_element_type=jnp.float32
    )
    finish_all(first)
    fill_grid(c_grid, c_pad)

    def conv_row(grid, x, y, flip):
        total = None
        for t in range(27):
            a, b, c = tap_offsets(t)
            w_at = 26 - t if flip else t
            term = grid[x + a, y + b, pl.ds(7 + c, ext_z), :] * depth_w[pl.ds(w_at, 1), :]
            total = term if total is None else total + term
        return total

    squares = jnp.zeros((8, chans), jnp.float32)
    for x in range(ext_x):
        def forward(y, acc):
            row = conv_row(c_grid, x, y, False)
            depth_out[pl.ds(pl.multiple_of((x * ext_y + y) * ext_z, ext_z), ext_z), :] = row
            return acc + fold8(row * row)
        squares = lax.fori_loop(0, ext_y, forward, squares)
    own_1[...] = squares
    spread_1 = spread_copies(own_1, slots_1, sem_c, sem_d, nodes)
    for copy in spread_1:
        copy.start()
    for copy in spread_1:
        copy.wait()
    total = own_1[...]
    for step in range(1, nodes):
        total = total + slots_1[step]
    square_sum = jnp.sum(total, axis=0, keepdims=True)
    gain = gain_ref[...]
    scale = lax.rsqrt(square_sum / count + eps)
    depth_all = depth_out[...]
    normed = (depth_all * (gain * scale)).astype(jnp.bfloat16).astype(jnp.float32)
    sigma = jax.nn.sigmoid(normed)
    activated = (normed * sigma).astype(jnp.bfloat16)
    slope = sigma * (1.0 + normed * (1.0 - sigma))
    g_normed = (g_act[...] * slope).astype(jnp.bfloat16).astype(jnp.float32)
    g_act[...] = g_normed
    own_2[...] = fold8(g_normed * depth_all)
    spread_2 = spread_copies(own_2, slots_2, sem_e, sem_f, nodes)
    for copy in spread_2:
        copy.start()
    mixed = coarse[...].reshape(cells, chans).astype(jnp.float32) + jnp.dot(
        activated, point_w[...], preferred_element_type=jnp.float32
    )
    out[...] = mixed.astype(jnp.bfloat16).reshape(coarse.shape)
    grad_point[...] = lax.dot_general(
        activated, up_rows, (((0,), (0,)), ((), ())), preferred_element_type=jnp.float32
    )
    grad_gain[...] = scale * jnp.sum(own_2[...], axis=0, keepdims=True)
    for copy in spread_2:
        copy.wait()
    total = own_2[...]
    for step in range(1, nodes):
        total = total + slots_2[step]
    cross = jnp.sum(total, axis=0, keepdims=True)
    g_in = gain * scale * g_act[...] - depth_out[...] * (
        gain * scale * scale * scale / count
    ) * cross
    g_own[...] = g_in.astype(jnp.bfloat16).reshape(coarse.shape)
    second = halo_copies(g_own, g_pad, sem_g, sem_h, nodes)
    start_all(second)
    g_pad[pl.ds(1, ext_x), pl.ds(1, ext_y)] = g_own[...]
    for a in range(3):
        sums = tuple(jnp.zeros((8, chans), jnp.float32) for _ in range(9))
        for x in range(ext_x):
            def taps(y, acc):
                g_row = g_own[x, y].astype(jnp.float32)
                return tuple(
                    acc[3 * b + c] + fold8(c_grid[x + a, y + b, pl.ds(7 + c, ext_z), :] * g_row)
                    for b in range(3)
                    for c in range(3)
                )
            sums = lax.fori_loop(0, ext_y, taps, sums)
        for k in range(9):
            grad_depth[pl.ds(9 * a + k, 1), :] = jnp.sum(sums[k], axis=0, keepdims=True)
    finish_all(second)
    fill_grid(g_grid, g_pad)
    for x in range(ext_x):
        def backward(y, carry):
            row = conv_row(g_grid, x, y, True).astype(jnp.bfloat16).astype(jnp.float32)
            grad_coarse[x, y] = (up[x, y].astype(jnp.float32) + row).astype(jnp.bfloat16)
            return carry
        lax.fori_loop(0, ext_y, backward, 0)


def coarse_level(coarse, up, depth_w, gain, point_w, nodes):
    ext_x, ext_y, ext_z, chans = coarse.shape
    cells = ext_x * ext_y * ext_z
    f32, bf16 = jnp.float32, jnp.bfloat16
    padded = (ext_x + 2, ext_y + 2, ext_z, chans)
    grid = (ext_x + 2, ext_y + 2, ext_z + 16, chans)
    dma = pltpu.SemaphoreType.DMA
    return pl.pallas_call(
        functools.partial(coarse_kernel, nodes),
        out_shape=(
            jax.ShapeDtypeStruct(coarse.shape, bf16),
            jax.ShapeDtypeStruct(coarse.shape, bf16),
            jax.ShapeDtypeStruct((chans, chans), f32),
            jax.ShapeDtypeStruct((27, chans), f32),
            jax.ShapeDtypeStruct((1, chans), f32),
        ),
        in_specs=[VMEM_SPEC] * 5,
        out_specs=(VMEM_SPEC,) * 5,
        scratch_shapes=[
            pltpu.VMEM(padded, bf16),
            pltpu.VMEM(padded, bf16),
            pltpu.VMEM(coarse.shape, bf16),
            pltpu.VMEM(grid, f32),
            pltpu.VMEM(grid, f32),
            pltpu.VMEM((cells, chans), f32),
            pltpu.VMEM((cells, chans), f32),
            pltpu.VMEM((8, chans), f32),
            pltpu.VMEM((8, chans), f32),
            pltpu.VMEM((nodes, 8, chans), f32),
            pltpu.VMEM((nodes, 8, chans), f32),
            dma((8,)), dma((8,)), dma((nodes,)), dma((nodes,)),
            dma((nodes,)), dma((nodes,)), dma((8,)), dma((8,)),
        ],
        compiler_params=pltpu.CompilerParams(
            collective_id=1, has_side_effects=True, vmem_limit_bytes=VMEM_BYTES
        ),
        name="coarse_level",
    )(coarse, up, depth_w, gain.reshape(1, chans), point_w)


def sum_kernel(nodes, src, out, got_1, got_2, got_3, part_1, part_2,
               core_send, core_recv, plane_send, plane_recv, line_send, line_recv):
    chunks, _, plane = src.shape[:3]
    width = nodes // 4
    me, dp = lax.axis_index("space"), lax.axis_index("dp")
    core = lax.rem(dp, 2)
    line, q = me // width, (dp // 2) * width + lax.rem(me, width)
    mate = (dp + 1 - 2 * core, me)

    def in_plane(step):
        at = lax.rem(q + step, plane)
        return at, ((at // width) * 2 + core, line * width + lax.rem(at, width))

    def in_line(step):
        at = lax.rem(line + step, 4)
        return at, (dp, at * width + lax.rem(me, width))

    barrier = pltpu.get_barrier_semaphore()
    peers = [mate] + [in_plane(s)[1] for s in range(1, plane)] + [in_line(s)[1] for s in range(1, 4)]
    for peer in peers:
        pl.semaphore_signal(barrier, inc=1, device_id=peer, device_id_type=MESH)
    pl.semaphore_wait(barrier, len(peers))

    def copy(source, dest, send_sem, recv_sem, peer):
        made = pltpu.make_async_remote_copy(
            src_ref=source, dst_ref=dest, send_sem=send_sem, recv_sem=recv_sem,
            device_id=peer, device_id_type=MESH,
        )
        made.start()
        return made

    f32, bf16 = jnp.float32, jnp.bfloat16
    sent = []

    def arrived(source, dest, send_sem, recv_sem, peer):
        pltpu.make_async_remote_copy(
            src_ref=source, dst_ref=dest, send_sem=send_sem, recv_sem=recv_sem,
            device_id=peer, device_id_type=MESH,
        ).wait_recv()

    step_1 = []
    for c in range(chunks):
        step_1.append(copy(src.at[c, 1 - core], got_1.at[c], core_send.at[0, c],
                           core_recv.at[0, c], mate))
    step_2 = []
    for c in range(chunks):
        step_1[c].wait()
        part_1[c] = (src[c, core].astype(f32) + got_1[c].astype(f32)).astype(bf16)
        row = []
        for s in range(1, plane):
            at, peer = in_plane(s)
            row.append(copy(part_1.at[c, at], got_2.at[c, s], plane_send.at[0, c, s],
                            plane_recv.at[0, c, s], peer))
        step_2.append(row)
    step_3 = []
    for c in range(chunks):
        for made in step_2[c]:
            made.wait()
        total = part_1[c, q].astype(f32)
        for s in range(1, plane):
            total = total + got_2[c, s].astype(f32)
        part_2[c] = total.astype(bf16)
        row = []
        for s in range(1, 4):
            at, peer = in_line(s)
            row.append(copy(part_2.at[c, at], got_3.at[c, s], line_send.at[0, c, s],
                            line_recv.at[0, c, s], peer))
        step_3.append(row)
    for c in range(chunks):
        for made in step_3[c]:
            made.wait()
        total = part_2[c, line].astype(f32)
        for s in range(1, 4):
            total = total + got_3[c, s].astype(f32)
        out[c, core, q, line] = total.astype(bf16)
        for s in range(1, 4):
            peer = in_line(s)[1]
            mine = out.at[c, core, q, line]
            sent.append(copy(mine, mine, line_send.at[1, c, s], line_recv.at[1, c, s], peer))
    for c in range(chunks):
        for s in range(1, 4):
            at, peer = in_line(4 - s)
            there = out.at[c, core, q, at]
            arrived(there, there, line_send.at[1, c, s], line_recv.at[1, c, s], peer)
        for s in range(1, plane):
            peer = in_plane(s)[1]
            mine = out.at[c, core, q]
            sent.append(copy(mine, mine, plane_send.at[1, c, s], plane_recv.at[1, c, s], peer))
    for c in range(chunks):
        for s in range(1, plane):
            at, peer = in_plane(plane - s)
            there = out.at[c, core, at]
            arrived(there, there, plane_send.at[1, c, s], plane_recv.at[1, c, s], peer)
        mine = out.at[c, core]
        sent.append(copy(mine, mine, core_send.at[1, c], core_recv.at[1, c], mate))
    for c in range(chunks):
        there = out.at[c, 1 - core]
        arrived(there, there, core_send.at[1, c], core_recv.at[1, c], mate)
    for made in sent:
        made.wait_send()


CHUNKS = 3


def sum_everywhere(grads, nodes, groups):
    plane = groups // 2 * (nodes // 4)
    lane = 128
    unit = CHUNKS * 2 * plane * 4 * 16
    flat = []
    for grad in grads:
        flat.append(grad.astype(jnp.bfloat16).reshape(-1, lane))
    rows = sum(part.shape[0] for part in flat)
    padded = -(-rows // unit) * unit
    if padded > rows:
        flat.append(jnp.zeros((padded - rows, lane), jnp.bfloat16))
    piece = padded // (CHUNKS * 2 * plane * 4)
    whole = jnp.concatenate(flat, axis=0).reshape(CHUNKS, 2, plane, 4, piece, lane)
    bf16, dma = jnp.bfloat16, pltpu.SemaphoreType.DMA
    summed = pl.pallas_call(
        functools.partial(sum_kernel, nodes),
        out_shape=jax.ShapeDtypeStruct(whole.shape, bf16),
        in_specs=[VMEM_SPEC],
        out_specs=VMEM_SPEC,
        scratch_shapes=[
            pltpu.VMEM((CHUNKS, plane, 4, piece, lane), bf16),
            pltpu.VMEM((CHUNKS, plane, 4, piece, lane), bf16),
            pltpu.VMEM((CHUNKS, 4, piece, lane), bf16),
            pltpu.VMEM((CHUNKS, plane, 4, piece, lane), bf16),
            pltpu.VMEM((CHUNKS, 4, piece, lane), bf16),
            dma((2, CHUNKS)), dma((2, CHUNKS)),
            dma((2, CHUNKS, plane)), dma((2, CHUNKS, plane)),
            dma((2, CHUNKS, 4)), dma((2, CHUNKS, 4)),
        ],
        compiler_params=pltpu.CompilerParams(
            collective_id=2, has_side_effects=True, vmem_limit_bytes=VMEM_BYTES
        ),
        name="sum_everywhere",
    )(whole).reshape(padded, lane)
    result, at = [], 0
    for grad in grads:
        count = grad.size // lane
        result.append(summed[at : at + count].astype(jnp.float32).reshape(grad.shape))
        at += count
    return result


def local(fields, conv_fine, conv_down, conv_depth, norm_gain, conv_point, upstream):
    nodes, groups = lax.axis_size("space"), lax.axis_size("dp")
    fine = fields[0, 0]
    brick_x, brick_y, brick_z, chan_fine = fine.shape
    fine_pad = jnp.pad(fine_halo(fine, nodes), ((0, 0), (0, 0), (1, 1), (0, 0)))
    pre_act = full_conv(fine_pad, conv_fine)
    act = jax.nn.silu(pre_act).astype(jnp.bfloat16)
    blocks = to_blocks(act.reshape(brick_x, brick_y, brick_z, chan_fine))
    coarse = jnp.dot(blocks, conv_down, preferred_element_type=jnp.float32).astype(jnp.bfloat16)
    up = upstream[0, 0]
    coarse_out, grad_coarse, grad_point, grad_depth, grad_gain = coarse_level(
        coarse.reshape(up.shape), up, conv_depth, norm_gain, conv_point, nodes
    )
    grad_coarse = grad_coarse.reshape(-1, up.shape[3])
    grad_down = lax.dot_general(
        blocks, grad_coarse, (((0,), (0,)), ((), ())), preferred_element_type=jnp.float32
    )
    grad_blocks = lax.dot_general(
        grad_coarse, conv_down, (((1,), (1,)), ((), ())), preferred_element_type=jnp.float32
    )
    grad_act_fine = from_blocks(grad_blocks, brick_x, brick_y, brick_z, chan_fine)
    grad_pre = (grad_act_fine * silu_slope(pre_act)).astype(jnp.bfloat16)
    grad_fine = tap_grads(fine_pad, grad_pre)
    totals = sum_everywhere(
        (grad_fine, grad_down, grad_depth, grad_gain.reshape(-1), grad_point), nodes, groups
    )
    return (coarse_out[None, None], *totals)


def solution(mesh):
    placed = (
        P("dp", "space", None, None, None, None),
        P(),
        P(),
        P(),
        P(),
        P(),
        P("dp", "space", None, None, None, None),
    )
    return jax.shard_map(
        local,
        mesh=mesh,
        in_specs=placed,
        out_specs=(P("dp", "space", None, None, None, None), P(), P(), P(), P(), P()),
        check_vma=False,
    )
```

```python
import functools
import jax
import jax.numpy as jnp
from jax import lax
from jax.experimental import pallas as pl
from jax.experimental.pallas import tpu as pltpu
from jax.sharding import PartitionSpec as P

eps = 1e-05
MESH = pl.DeviceIdType.MESH
OFFSETS = [(dx, dy) for dx in (-1, 0, 1) for dy in (-1, 0, 1) if (dx, dy) != (0, 0)]
VMEM_SPEC = pl.BlockSpec(memory_space=pltpu.VMEM)
VMEM_BYTES = 48 * 1024 * 1024


def tap_offsets(tap_index):
    return (tap_index // 9, tap_index // 3 % 3, tap_index % 3)


def edge_of(delta, ext):
    return {-1: pl.ds(0, 1), 0: pl.ds(0, ext), 1: pl.ds(ext - 1, 1)}[delta]


def rim_of(delta, ext):
    return {-1: pl.ds(0, 1), 0: pl.ds(1, ext), 1: pl.ds(ext + 1, 1)}[delta]


def halo_copies(src, dst, send_sem, recv_sem, nodes):
    me, dp = lax.axis_index("space"), lax.axis_index("dp")
    ext_x, ext_y = src.shape[0], src.shape[1]
    pos_x, pos_y = me // 4, lax.rem(me, 4)
    result = []
    for k, (dx, dy) in enumerate(OFFSETS):
        exists = jnp.logical_and(
            jnp.logical_and(pos_x + dx >= 0, pos_x + dx < nodes // 4),
            jnp.logical_and(pos_y + dy >= 0, pos_y + dy < 4),
        )
        source = src.at[edge_of(dx, ext_x), edge_of(dy, ext_y)]
        peer = (dp, me + 4 * dx + dy)
        send = pltpu.make_async_remote_copy(
            src_ref=source,
            dst_ref=dst.at[rim_of(-dx, ext_x), rim_of(-dy, ext_y)],
            send_sem=send_sem.at[k],
            recv_sem=recv_sem.at[7 - k],
            device_id=peer,
            device_id_type=MESH,
        )
        arrival = pltpu.make_async_remote_copy(
            src_ref=source,
            dst_ref=dst.at[rim_of(dx, ext_x), rim_of(dy, ext_y)],
            send_sem=send_sem.at[k],
            recv_sem=recv_sem.at[k],
            device_id=peer,
            device_id_type=MESH,
        )
        result.append((exists, send, arrival))
    return result


def start_all(copies):
    for k in (0, 1, 2, 5, 6, 7, 3, 4):
        exists, send, _ = copies[k]
        pl.when(exists)(send.start)


def finish(copies, which):
    for k in which:
        exists, _, arrival = copies[k]
        pl.when(exists)(arrival.wait)


BESIDE, BEYOND = (3, 4), (0, 1, 2, 5, 6, 7)


def fold8(rows):
    return jnp.sum(rows.reshape(rows.shape[0] // 8, 8, rows.shape[1]), axis=0)


def spread_copies(own, slots, send_sem, recv_sem, nodes):
    me, dp = lax.axis_index("space"), lax.axis_index("dp")
    return [
        pltpu.make_async_remote_copy(
            src_ref=own,
            dst_ref=slots.at[step],
            send_sem=send_sem.at[step],
            recv_sem=recv_sem.at[step],
            device_id=(dp, lax.rem(me + step, nodes)),
            device_id_type=MESH,
        )
        for step in range(1, nodes)
    ]


def fill_grid(grid, padded, plane):
    ext_z = padded.shape[2]
    side = jnp.zeros((grid.shape[1], 8, grid.shape[3]), jnp.float32)
    grid[plane, :, pl.ds(0, 8)] = side
    grid[plane, :, pl.ds(8 + ext_z, 8)] = side
    grid[plane, :, pl.ds(8, ext_z)] = padded[plane].astype(jnp.float32)


CHUNKS = 3
LANE = 128


class Summing:
    def __init__(self, nodes, groups, src, out, bufs, sems):
        self.src, self.out = src, out
        self.got_1, self.got_2, self.got_3, self.part_1, self.part_2 = bufs
        self.core_send, self.core_recv, self.plane_send, self.plane_recv, self.line_send, self.line_recv = sems
        self.width = nodes // 4
        self.plane = groups // 2 * self.width
        self.me, self.dp = lax.axis_index("space"), lax.axis_index("dp")
        self.core = lax.rem(self.dp, 2)
        self.line = self.me // self.width
        self.q = (self.dp // 2) * self.width + lax.rem(self.me, self.width)
        self.mate = (self.dp + 1 - 2 * self.core, self.me)
        self.piece = src.shape[0] // (CHUNKS * 2 * self.plane * 4)
        self.made, self.sent = {}, []

    def in_plane(self, step):
        at = lax.rem(self.q + step, self.plane)
        return at, (
            (at // self.width) * 2 + self.core,
            self.line * self.width + lax.rem(at, self.width),
        )

    def in_line(self, step):
        at = lax.rem(self.line + step, 4)
        return at, (self.dp, at * self.width + lax.rem(self.me, self.width))

    def rows(self, c, h, q=None, line=None):
        count = self.piece
        at = (c * 2 + h) * self.plane
        if q is None:
            at, count = at * 4, count * self.plane * 4
        elif line is None:
            at, count = (at + q) * 4, count * 4
        else:
            at = (at + q) * 4 + line
        return pl.ds(pl.multiple_of(at * self.piece, 16), count)

    def copy(self, source, dest, send_sem, recv_sem, peer):
        return pltpu.make_async_remote_copy(
            src_ref=source, dst_ref=dest, send_sem=send_sem, recv_sem=recv_sem,
            device_id=peer, device_id_type=MESH,
        )

    def push(self, key, *args):
        made = self.copy(*args)
        made.start()
        self.made.setdefault(key, []).append(made)

    def give(self, dest, *args):
        made = self.copy(dest, dest, *args)
        made.start()
        self.sent.append(made)

    def taken(self, dest, *args):
        self.copy(dest, dest, *args).wait_recv()

    def finished(self, key):
        for made in self.made[key]:
            made.wait()

    def step_1(self, c):
        self.push((1, c), self.src.at[self.rows(c, 1 - self.core)], self.got_1.at[c],
                  self.core_send.at[0, c], self.core_recv.at[0, c], self.mate)

    def step_2(self, c):
        self.finished((1, c))
        own = self.src[self.rows(c, self.core), :].astype(jnp.float32)
        self.part_1[c] = (own + self.got_1[c].astype(jnp.float32)).astype(jnp.bfloat16)
        count = 4 * self.piece
        for s in range(1, self.plane):
            at, peer = self.in_plane(s)
            self.push((2, c), self.part_1.at[c, pl.ds(pl.multiple_of(at * count, 16), count)],
                      self.got_2.at[c, s], self.plane_send.at[0, c, s],
                      self.plane_recv.at[0, c, s], peer)

    def step_3(self, c):
        self.finished((2, c))
        count = 4 * self.piece
        total = self.part_1[c, pl.ds(pl.multiple_of(self.q * count, 16), count), :].astype(jnp.float32)
        for s in range(1, self.plane):
            total = total + self.got_2[c, s].astype(jnp.float32)
        self.part_2[c] = total.astype(jnp.bfloat16)
        for s in range(1, 4):
            at, peer = self.in_line(s)
            self.push((3, c),
                      self.part_2.at[c, pl.ds(pl.multiple_of(at * self.piece, 16), self.piece)],
                      self.got_3.at[c, s], self.line_send.at[0, c, s],
                      self.line_recv.at[0, c, s], peer)

    def step_4(self, c):
        self.finished((3, c))
        total = self.part_2[
            c, pl.ds(pl.multiple_of(self.line * self.piece, 16), self.piece), :
        ].astype(jnp.float32)
        for s in range(1, 4):
            total = total + self.got_3[c, s].astype(jnp.float32)
        mine = self.rows(c, self.core, self.q, self.line)
        self.out[mine, :] = total.astype(jnp.bfloat16)
        for s in range(1, 4):
            self.give(self.out.at[mine], self.line_send.at[1, c, s], self.line_recv.at[1, c, s],
                      self.in_line(s)[1])

    def step_5(self, c):
        for s in range(1, 4):
            at, peer = self.in_line(4 - s)
            self.taken(self.out.at[self.rows(c, self.core, self.q, at)],
                       self.line_send.at[1, c, s], self.line_recv.at[1, c, s], peer)
        for s in range(1, self.plane):
            self.give(self.out.at[self.rows(c, self.core, self.q)], self.plane_send.at[1, c, s],
                      self.plane_recv.at[1, c, s], self.in_plane(s)[1])

    def step_6(self, c):
        for s in range(1, self.plane):
            at, peer = self.in_plane(self.plane - s)
            self.taken(self.out.at[self.rows(c, self.core, at)],
                       self.plane_send.at[1, c, s], self.plane_recv.at[1, c, s], peer)
        self.give(self.out.at[self.rows(c, self.core)], self.core_send.at[1, c],
                  self.core_recv.at[1, c], self.mate)

    def step_7(self, c):
        self.taken(self.out.at[self.rows(c, 1 - self.core)], self.core_send.at[1, c],
                   self.core_recv.at[1, c], self.mate)

    def close(self):
        for made in self.sent:
            made.wait_send()


def greet(nodes, groups):
    me, dp = lax.axis_index("space"), lax.axis_index("dp")
    width, core = nodes // 4, lax.rem(dp, 2)
    peers = [(dp, lax.rem(me + step, nodes)) for step in range(1, nodes)]
    peers.append((dp + 1 - 2 * core, me))
    for step in range(1, groups // 2):
        other = lax.rem(dp // 2 + step, groups // 2) * 2 + core
        for w in range(width):
            peers.append((other, (me // width) * width + w))
    barrier = pltpu.get_barrier_semaphore()
    for peer in peers:
        pl.semaphore_signal(barrier, inc=1, device_id=peer, device_id_type=MESH)
    pl.semaphore_wait(barrier, len(peers))


GROUP = 4


def level_kernel(
    nodes, groups, fine, w_fine, w_down, depth_w, gain_ref, point_w, up,
    out, out_fine, out_down, out_depth, out_gain, out_point,
    f_pad, stack, pre, act, blocks, g_blocks, g_pre_t,
    coarse, c_pad, g_pad, g_own, g_coarse, c_grid, g_grid, depth_out, g_act, small,
    own_1, own_2, slots_1, slots_2, flat, summed,
    got_1, got_2, got_3, part_1, part_2,
    sem_i, sem_j, sem_a, sem_b, sem_c, sem_d, sem_e, sem_f, sem_g, sem_h,
    *sum_sems,
):
    f32, bf16 = jnp.float32, jnp.bfloat16
    fine_x, fine_y, fine_z, chan = fine.shape
    ext_x, ext_y, ext_z, chans = coarse.shape
    cells = ext_x * ext_y * ext_z
    count = nodes * cells
    f_pad[...] = jnp.zeros_like(f_pad)
    c_pad[...] = jnp.zeros_like(c_pad)
    g_pad[...] = jnp.zeros_like(g_pad)
    greet(nodes, groups)
    total_of = Summing(nodes, groups, flat, summed, (got_1, got_2, got_3, part_1, part_2), sum_sems)
    halo = halo_copies(fine, f_pad, sem_i, sem_j, nodes)
    start_all(halo)
    f_pad[pl.ds(1, fine_x), pl.ds(1, fine_y)] = fine[...]

    def stack_planes(planes):
        spot = lax.broadcasted_iota(jnp.int32, (fine_z, chan), 0)

        def stack_row(y, carry):
            for p in planes:
                row = f_pad[p, y]
                wide = row.astype(f32)
                before = jnp.where(spot == 0, 0.0, pltpu.roll(wide, 1, 0))
                after = jnp.where(spot == fine_z - 1, 0.0, pltpu.roll(wide, fine_z - 1, 0))
                stack[p, y, :, pl.ds(0, chan)] = before.astype(bf16)
                stack[p, y, :, pl.ds(chan, chan)] = row
                stack[p, y, :, pl.ds(2 * chan, chan)] = after.astype(bf16)
            return carry

        lax.fori_loop(0, fine_y + 2, stack_row, 0)

    def conv_planes(planes, first):
        size = GROUP * fine_z

        def conv_group(y_group, carry):
            for x in range(fine_x):
                total = None
                for a in range(3):
                    if x + a not in planes:
                        continue
                    for b in range(3):
                        rows = stack[x + a, pl.ds(y_group * GROUP + b, GROUP)].reshape(size, 3 * chan)
                        term = jnp.dot(
                            rows,
                            w_fine[pl.ds((3 * a + b) * 3 * chan, 3 * chan), :],
                            preferred_element_type=f32,
                        )
                        total = term if total is None else total + term
                at = pl.ds(pl.multiple_of(x * fine_y * fine_z + y_group * size, size), size)
                if total is not None:
                    pre[at, :] = total if first else pre[at, :] + total
            return carry

        lax.fori_loop(0, fine_y // GROUP, conv_group, 0)

    inner, outer = list(range(1, fine_x + 1)), [0, fine_x + 1]
    finish(halo, BESIDE)
    stack_planes(inner)
    conv_planes(inner, True)
    finish(halo, BEYOND)
    stack_planes(outer)
    conv_planes(outer, False)

    def fine_rows(x, y):
        return (x * fine_y + y) * fine_z

    def activate(y, carry):
        for x in range(fine_x):
            at = pl.ds(pl.multiple_of(fine_rows(x, 2 * y), 2 * fine_z), 2 * fine_z)
            value = pre[at, :]
            act[at, :] = (value * jax.nn.sigmoid(value)).astype(bf16).astype(f32)
            for j in range(2):
                for k in range(2):
                    off = 4 * (x % 2) + 2 * j + k
                    part = act[pl.ds(fine_rows(x, 2 * y + j) + k, ext_z, stride=2), :]
                    rows = pl.ds(pl.multiple_of((x // 2 * ext_y + y) * ext_z, ext_z), ext_z)
                    blocks[rows, pl.ds(off * chan, chan)] = part.astype(bf16)
        return carry

    lax.fori_loop(0, ext_y, activate, 0)
    coarse[...] = (
        jnp.dot(blocks[...], w_down[...], preferred_element_type=f32)
        .astype(bf16)
        .reshape(coarse.shape)
    )
    first = halo_copies(coarse, c_pad, sem_a, sem_b, nodes)
    start_all(first)
    c_pad[pl.ds(1, ext_x), pl.ds(1, ext_y)] = coarse[...]
    up_rows = up[...].reshape(cells, chans)
    g_act[...] = lax.dot_general(
        up_rows, point_w[...], (((1,), (1,)), ((), ())), preferred_element_type=f32
    )

    def conv_row(grid, x, y, flip, planes):
        total = None
        for t in range(27):
            a, b, c = tap_offsets(t)
            if x + a not in planes:
                continue
            w_at = 26 - t if flip else t
            term = grid[x + a, y + b, pl.ds(7 + c, ext_z), :] * depth_w[pl.ds(w_at, 1), :]
            total = term if total is None else total + term
        return total

    def cell_rows(x, y):
        return pl.ds(pl.multiple_of((x * ext_y + y) * ext_z, ext_z), ext_z)

    middle, ends = list(range(1, ext_x + 1)), [0, ext_x + 1]
    finish(first, BESIDE)
    for p in middle:
        fill_grid(c_grid, c_pad, p)

    def forward_own(y, carry):
        for x in range(ext_x):
            depth_out[cell_rows(x, y), :] = conv_row(c_grid, x, y, False, middle)
        return carry

    lax.fori_loop(0, ext_y, forward_own, 0)

    def slopes(y, carry):
        for x in range(fine_x):
            at = pl.ds(pl.multiple_of(fine_rows(x, 2 * y), 2 * fine_z), 2 * fine_z)
            value = pre[at, :]
            sigma = jax.nn.sigmoid(value)
            pre[at, :] = sigma * (1.0 + value * (1.0 - sigma))
        return carry

    lax.fori_loop(0, ext_y, slopes, 0)
    finish(first, BEYOND)
    for p in ends:
        fill_grid(c_grid, c_pad, p)

    def forward(y, acc):
        for x in range(ext_x):
            row = depth_out[cell_rows(x, y), :]
            rest = conv_row(c_grid, x, y, False, ends)
            row = row if rest is None else row + rest
            depth_out[cell_rows(x, y), :] = row
            acc = acc + fold8(row * row)
        return acc

    own_1[...] = lax.fori_loop(0, ext_y, forward, jnp.zeros((8, chans), f32))
    spread_1 = spread_copies(own_1, slots_1, sem_c, sem_d, nodes)
    for copy in spread_1:
        copy.start()
    for copy in spread_1:
        copy.wait()
    total = own_1[...]
    for step in range(1, nodes):
        total = total + slots_1[step]
    square_sum = jnp.sum(total, axis=0, keepdims=True)
    gain = gain_ref[...]
    scale = lax.rsqrt(square_sum / count + eps)
    depth_all = depth_out[...]
    normed = (depth_all * (gain * scale)).astype(bf16).astype(f32)
    sigma = jax.nn.sigmoid(normed)
    activated = (normed * sigma).astype(bf16)
    slope = sigma * (1.0 + normed * (1.0 - sigma))
    g_normed = (g_act[...] * slope).astype(bf16).astype(f32)
    g_act[...] = g_normed
    own_2[...] = fold8(g_normed * depth_all)
    spread_2 = spread_copies(own_2, slots_2, sem_e, sem_f, nodes)
    for copy in spread_2:
        copy.start()
    mixed = coarse[...].reshape(cells, chans).astype(f32) + jnp.dot(
        activated, point_w[...], preferred_element_type=f32
    )
    out[...] = mixed.astype(bf16).reshape(coarse.shape)
    down_rows, point_rows = 8 * chan, chans
    at_point, at_small = 2 * down_rows, 2 * down_rows + 2 * point_rows
    at_fine = at_small + 64
    in_point = lax.dot_general(
        activated, up_rows, (((0,), (0,)), ((), ())), preferred_element_type=f32
    ).astype(bf16)
    flat[pl.ds(at_point, point_rows), :] = in_point[:, :LANE]
    flat[pl.ds(at_point + point_rows, point_rows), :] = in_point[:, LANE:]
    small[...] = jnp.zeros_like(small)
    small[pl.ds(27, 1), :] = scale * jnp.sum(own_2[...], axis=0, keepdims=True)
    for copy in spread_2:
        copy.wait()
    total = own_2[...]
    for step in range(1, nodes):
        total = total + slots_2[step]
    cross = jnp.sum(total, axis=0, keepdims=True)
    g_in = gain * scale * g_act[...] - depth_out[...] * (
        gain * scale * scale * scale / count
    ) * cross
    g_own[...] = g_in.astype(bf16).reshape(coarse.shape)
    second = halo_copies(g_own, g_pad, sem_g, sem_h, nodes)
    start_all(second)
    g_pad[pl.ds(1, ext_x), pl.ds(1, ext_y)] = g_own[...]
    for a in range(3):
        def taps(y, acc):
            for x in range(ext_x):
                g_row = g_own[x, y].astype(f32)
                acc = tuple(
                    acc[3 * b + c] + fold8(c_grid[x + a, y + b, pl.ds(7 + c, ext_z), :] * g_row)
                    for b in range(3)
                    for c in range(3)
                )
            return acc
        sums = tuple(jnp.zeros((8, chans), f32) for _ in range(9))
        sums = lax.fori_loop(0, ext_y, taps, sums)
        for k in range(9):
            small[pl.ds(9 * a + k, 1), :] = jnp.sum(sums[k], axis=0, keepdims=True)
    small_16 = small[...].astype(bf16)
    flat[pl.ds(at_small, 32), :] = small_16[:, :LANE]
    flat[pl.ds(at_small + 32, 32), :] = small_16[:, LANE:]
    finish(second, BESIDE + BEYOND)
    for p in middle + ends:
        fill_grid(g_grid, g_pad, p)

    def backward(y, carry):
        for x in range(ext_x):
            row = conv_row(g_grid, x, y, True, middle + ends).astype(bf16).astype(f32)
            g_coarse[cell_rows(x, y), :] = (up[x, y].astype(f32) + row).astype(bf16)
        return carry

    lax.fori_loop(0, ext_y, backward, 0)
    in_down = lax.dot_general(
        blocks[...], g_coarse[...], (((0,), (0,)), ((), ())), preferred_element_type=f32
    ).astype(bf16)
    flat[pl.ds(0, down_rows), :] = in_down[:, :LANE]
    flat[pl.ds(down_rows, down_rows), :] = in_down[:, LANE:]
    total_of.step_1(0)
    g_blocks[...] = lax.dot_general(
        g_coarse[...], w_down[...], (((1,), (1,)), ((), ())), preferred_element_type=f32
    )

    def spread_back(y, carry):
        for x in range(fine_x):
            for j in range(2):
                for k in range(2):
                    off = 4 * (x % 2) + 2 * j + k
                    part = g_blocks[cell_rows(x // 2, y), pl.ds(off * chan, chan)]
                    act[pl.ds(fine_rows(x, 2 * y + j) + k, ext_z, stride=2), :] = part
            start = pl.multiple_of(fine_rows(x, 2 * y), 2 * fine_z)
            at = pl.ds(start, 2 * fine_z)
            g_pre_t[:, at] = (act[at, :] * pre[at, :]).T.astype(bf16)
        return carry

    lax.fori_loop(0, ext_y, spread_back, 0)

    def weight_grads(low, high):
        def one(at, carry):
            rows = stack[pl.ds(at // 3, fine_x), pl.ds(lax.rem(at, 3), fine_y)]
            turned = jnp.dot(
                g_pre_t[...],
                rows.reshape(fine_x * fine_y * fine_z, 3 * chan),
                preferred_element_type=f32,
            )
            for c in range(3):
                start = pl.multiple_of(at_fine + (3 * at + c) * chan, 16)
                flat[pl.ds(start, chan), :] = turned[:, c * chan : (c + 1) * chan].T.astype(bf16)
            return carry

        lax.fori_loop(low, high, one, 0)

    used = at_fine + 27 * chan
    if used < flat.shape[0]:
        flat[pl.ds(used, flat.shape[0] - used), :] = jnp.zeros(
            (flat.shape[0] - used, LANE), bf16
        )
    split = min(9, -(-(2 * (flat.shape[0] // CHUNKS) - at_fine) // (3 * chan)))
    weight_grads(0, split)
    total_of.step_1(1)
    total_of.step_2(0)
    weight_grads(split, 9)
    total_of.step_1(2)
    for c in range(1, CHUNKS):
        total_of.step_2(c)
        total_of.step_3(c - 1)
    total_of.step_4(0)
    total_of.step_3(CHUNKS - 1)
    total_of.step_5(0)
    for c in range(1, CHUNKS):
        total_of.step_4(c)
    for c in range(1, CHUNKS):
        total_of.step_5(c)
    for c in range(CHUNKS):
        total_of.step_6(c)
    total_of.step_7(0)
    out_down[:, pl.ds(0, LANE)] = summed[pl.ds(0, down_rows), :].astype(f32)
    out_down[:, pl.ds(LANE, LANE)] = summed[pl.ds(down_rows, down_rows), :].astype(f32)
    for c in range(1, CHUNKS):
        total_of.step_7(c)
    for part in range(2):
        lanes = pl.ds(part * LANE, LANE)
        out_point[:, lanes] = summed[
            pl.ds(at_point + part * point_rows, point_rows), :
        ].astype(f32)
        small[:, lanes] = summed[pl.ds(at_small + 32 * part, 32), :].astype(f32)
    out_depth[...] = small[pl.ds(0, 27), :]
    out_gain[...] = small[pl.ds(27, 1), :]
    out_fine[...] = summed[pl.ds(at_fine, 27 * chan), :].astype(f32)
    total_of.close()


def whole_level(fine, w_fine, w_down, depth_w, gain, point_w, up, nodes, groups):
    f32, bf16, dma = jnp.float32, jnp.bfloat16, pltpu.SemaphoreType.DMA
    fine_x, fine_y, fine_z, chan = fine.shape
    ext_x, ext_y, ext_z, chans = up.shape
    cells, fine_cells = ext_x * ext_y * ext_z, fine_x * fine_y * fine_z
    padded = (ext_x + 2, ext_y + 2, ext_z, chans)
    grid = (ext_x + 2, ext_y + 2, ext_z + 16, chans)
    plane = groups // 2 * (nodes // 4)
    unit = CHUNKS * 2 * plane * 4 * 16
    rows = 16 * chan + 2 * chans + 64 + 27 * chan
    rows = -(-rows // unit) * unit
    piece = rows // (CHUNKS * 2 * plane * 4)
    return pl.pallas_call(
        functools.partial(level_kernel, nodes, groups),
        out_shape=(
            jax.ShapeDtypeStruct(up.shape, bf16),
            jax.ShapeDtypeStruct((27 * chan, chan), f32),
            jax.ShapeDtypeStruct((8 * chan, chans), f32),
            jax.ShapeDtypeStruct((27, chans), f32),
            jax.ShapeDtypeStruct((1, chans), f32),
            jax.ShapeDtypeStruct((chans, chans), f32),
        ),
        in_specs=[VMEM_SPEC] * 7,
        out_specs=(VMEM_SPEC,) * 6,
        scratch_shapes=[
            pltpu.VMEM((fine_x + 2, fine_y + 2, fine_z, chan), bf16),
            pltpu.VMEM((fine_x + 2, fine_y + 2, fine_z, 3 * chan), bf16),
            pltpu.VMEM((fine_cells, chan), f32),
            pltpu.VMEM((fine_cells, chan), f32),
            pltpu.VMEM((cells, 8 * chan), bf16),
            pltpu.VMEM((cells, 8 * chan), f32),
            pltpu.VMEM((chan, fine_cells), bf16),
            pltpu.VMEM(up.shape, bf16),
            pltpu.VMEM(padded, bf16),
            pltpu.VMEM(padded, bf16),
            pltpu.VMEM(up.shape, bf16),
            pltpu.VMEM((cells, chans), bf16),
            pltpu.VMEM(grid, f32),
            pltpu.VMEM(grid, f32),
            pltpu.VMEM((cells, chans), f32),
            pltpu.VMEM((cells, chans), f32),
            pltpu.VMEM((32, chans), f32),
            pltpu.VMEM((8, chans), f32),
            pltpu.VMEM((8, chans), f32),
            pltpu.VMEM((nodes, 8, chans), f32),
            pltpu.VMEM((nodes, 8, chans), f32),
            pltpu.VMEM((rows, LANE), bf16),
            pltpu.VMEM((rows, LANE), bf16),
            pltpu.VMEM((CHUNKS, plane * 4 * piece, LANE), bf16),
            pltpu.VMEM((CHUNKS, plane, 4 * piece, LANE), bf16),
            pltpu.VMEM((CHUNKS, 4, piece, LANE), bf16),
            pltpu.VMEM((CHUNKS, plane * 4 * piece, LANE), bf16),
            pltpu.VMEM((CHUNKS, 4 * piece, LANE), bf16),
            dma((8,)), dma((8,)),
            dma((8,)), dma((8,)), dma((nodes,)), dma((nodes,)),
            dma((nodes,)), dma((nodes,)), dma((8,)), dma((8,)),
            dma((2, CHUNKS)), dma((2, CHUNKS)),
            dma((2, CHUNKS, plane)), dma((2, CHUNKS, plane)),
            dma((2, CHUNKS, 4)), dma((2, CHUNKS, 4)),
        ],
        compiler_params=pltpu.CompilerParams(
            collective_id=0, has_side_effects=True, vmem_limit_bytes=VMEM_BYTES
        ),
        name="whole_level",
    )(fine, w_fine.reshape(-1, w_fine.shape[2]), w_down, depth_w, gain.reshape(1, chans), point_w, up)


def local(fields, conv_fine, conv_down, conv_depth, norm_gain, conv_point, upstream):
    nodes, groups = lax.axis_size("space"), lax.axis_size("dp")
    coarse_out, fine, down, depth, gain, point = whole_level(
        fields[0, 0], conv_fine, conv_down, conv_depth, norm_gain, conv_point, upstream[0, 0],
        nodes, groups,
    )
    return (
        coarse_out[None, None], fine.reshape(conv_fine.shape), down, depth, gain.reshape(-1), point
    )


def solution(mesh):
    placed = (
        P("dp", "space", None, None, None, None),
        P(),
        P(),
        P(),
        P(),
        P(),
        P("dp", "space", None, None, None, None),
    )
    return jax.shard_map(
        local,
        mesh=mesh,
        in_specs=placed,
        out_specs=(P("dp", "space", None, None, None, None), P(), P(), P(), P(), P()),
        check_vma=False,
    )
```

```python
import functools
import jax
import jax.numpy as jnp
from jax import lax
from jax.experimental import pallas as pl
from jax.experimental.pallas import tpu as pltpu
from jax.sharding import PartitionSpec as P

eps = 1e-05
MESH = pl.DeviceIdType.MESH
OFFSETS = [(dx, dy) for dx in (-1, 0, 1) for dy in (-1, 0, 1) if (dx, dy) != (0, 0)]
VMEM_SPEC = pl.BlockSpec(memory_space=pltpu.VMEM)
ANY_SPEC = pl.BlockSpec(memory_space=pl.ANY)
VMEM_BYTES = 61 * 1024 * 1024


def tap_offsets(tap_index):
    return (tap_index // 9, tap_index // 3 % 3, tap_index % 3)


def edge_of(delta, ext):
    return {-1: pl.ds(0, 1), 0: pl.ds(0, ext), 1: pl.ds(ext - 1, 1)}[delta]


def rim_of(delta, ext):
    return {-1: pl.ds(0, 1), 0: pl.ds(1, ext), 1: pl.ds(ext + 1, 1)}[delta]


def halo_copies(src, dst, send_sem, recv_sem, nodes):
    me, dp = lax.axis_index("space"), lax.axis_index("dp")
    ext_x, ext_y = src.shape[0], src.shape[1]
    pos_x, pos_y = me // 4, lax.rem(me, 4)
    result = []
    for k, (dx, dy) in enumerate(OFFSETS):
        exists = jnp.logical_and(
            jnp.logical_and(pos_x + dx >= 0, pos_x + dx < nodes // 4),
            jnp.logical_and(pos_y + dy >= 0, pos_y + dy < 4),
        )
        source = src.at[edge_of(dx, ext_x), edge_of(dy, ext_y)]
        peer = (dp, me + 4 * dx + dy)
        send = pltpu.make_async_remote_copy(
            src_ref=source,
            dst_ref=dst.at[rim_of(-dx, ext_x), rim_of(-dy, ext_y)],
            send_sem=send_sem.at[k],
            recv_sem=recv_sem.at[7 - k],
            device_id=peer,
            device_id_type=MESH,
        )
        arrival = pltpu.make_async_remote_copy(
            src_ref=source,
            dst_ref=dst.at[rim_of(dx, ext_x), rim_of(dy, ext_y)],
            send_sem=send_sem.at[k],
            recv_sem=recv_sem.at[k],
            device_id=peer,
            device_id_type=MESH,
        )
        result.append((exists, send, arrival))
    return result


def start_all(copies):
    for k in (3, 4, 1, 6, 0, 2, 5, 7):
        exists, send, _ = copies[k]
        pl.when(exists)(send.start)


def finish(copies, which):
    for k in which:
        exists, _, arrival = copies[k]
        pl.when(exists)(arrival.wait)


BESIDE, BEYOND = (3, 4), (0, 1, 2, 5, 6, 7)


def fold8(rows):
    return jnp.sum(rows.reshape(rows.shape[0] // 8, 8, rows.shape[1]), axis=0)


def spread_copies(own, slots, send_sem, recv_sem, nodes):
    me, dp = lax.axis_index("space"), lax.axis_index("dp")
    return [
        pltpu.make_async_remote_copy(
            src_ref=own,
            dst_ref=slots.at[step],
            send_sem=send_sem.at[step],
            recv_sem=recv_sem.at[step],
            device_id=(dp, lax.rem(me + step, nodes)),
            device_id_type=MESH,
        )
        for step in range(1, nodes)
    ]


def fill_grid(grid, padded, plane):
    ext_z = padded.shape[2]
    side = jnp.zeros((grid.shape[1], 8, grid.shape[3]), jnp.float32)
    grid[plane, :, pl.ds(0, 8)] = side
    grid[plane, :, pl.ds(8 + ext_z, 8)] = side
    grid[plane, :, pl.ds(8, ext_z)] = padded[plane].astype(jnp.float32)


CHUNKS = 3
LANE = 128


class Summing:
    def __init__(self, nodes, groups, src, out, bufs, sems):
        self.src, self.out = src, out
        self.got_1, self.got_2, self.got_3, self.part_1, self.part_2 = bufs
        self.core_send, self.core_recv, self.plane_send, self.plane_recv, self.line_send, self.line_recv = sems
        self.width = nodes // 4
        self.plane = groups // 2 * self.width
        self.me, self.dp = lax.axis_index("space"), lax.axis_index("dp")
        self.core = lax.rem(self.dp, 2)
        self.line = self.me // self.width
        self.q = (self.dp // 2) * self.width + lax.rem(self.me, self.width)
        self.mate = (self.dp + 1 - 2 * self.core, self.me)
        self.piece = src.shape[0] // (CHUNKS * 2 * self.plane * 4)
        self.made, self.sent = {}, []

    def in_plane(self, step):
        at = lax.rem(self.q + step, self.plane)
        return at, (
            (at // self.width) * 2 + self.core,
            self.line * self.width + lax.rem(at, self.width),
        )

    def in_line(self, step):
        at = lax.rem(self.line + step, 4)
        return at, (self.dp, at * self.width + lax.rem(self.me, self.width))

    def rows(self, c, h, q=None, line=None):
        count = self.piece
        at = (c * 2 + h) * self.plane
        if q is None:
            at, count = at * 4, count * self.plane * 4
        elif line is None:
            at, count = (at + q) * 4, count * 4
        else:
            at = (at + q) * 4 + line
        return pl.ds(pl.multiple_of(at * self.piece, 16), count)

    def copy(self, source, dest, send_sem, recv_sem, peer):
        return pltpu.make_async_remote_copy(
            src_ref=source, dst_ref=dest, send_sem=send_sem, recv_sem=recv_sem,
            device_id=peer, device_id_type=MESH,
        )

    def push(self, key, *args):
        made = self.copy(*args)
        made.start()
        self.made.setdefault(key, []).append(made)

    def give(self, dest, *args):
        made = self.copy(dest, dest, *args)
        made.start()
        self.sent.append(made)

    def taken(self, dest, *args):
        self.copy(dest, dest, *args).wait_recv()

    def finished(self, key):
        for made in self.made[key]:
            made.wait()

    def step_1(self, c):
        self.push((1, c), self.src.at[self.rows(c, 1 - self.core)], self.got_1.at[c],
                  self.core_send.at[0, c], self.core_recv.at[0, c], self.mate)

    def step_2(self, c):
        self.finished((1, c))
        own = self.src[self.rows(c, self.core), :].astype(jnp.float32)
        self.part_1[c] = (own + self.got_1[c].astype(jnp.float32)).astype(jnp.bfloat16)
        count = 4 * self.piece
        for s in range(1, self.plane):
            at, peer = self.in_plane(s)
            self.push((2, c), self.part_1.at[c, pl.ds(pl.multiple_of(at * count, 16), count)],
                      self.got_2.at[c, s], self.plane_send.at[0, c, s],
                      self.plane_recv.at[0, c, s], peer)

    def step_3(self, c):
        self.finished((2, c))
        count = 4 * self.piece
        total = self.part_1[c, pl.ds(pl.multiple_of(self.q * count, 16), count), :].astype(jnp.float32)
        for s in range(1, self.plane):
            total = total + self.got_2[c, s].astype(jnp.float32)
        self.part_2[c] = total.astype(jnp.bfloat16)
        for s in range(1, 4):
            at, peer = self.in_line(s)
            self.push((3, c),
                      self.part_2.at[c, pl.ds(pl.multiple_of(at * self.piece, 16), self.piece)],
                      self.got_3.at[c, s], self.line_send.at[0, c, s],
                      self.line_recv.at[0, c, s], peer)

    def step_4(self, c):
        self.finished((3, c))
        total = self.part_2[
            c, pl.ds(pl.multiple_of(self.line * self.piece, 16), self.piece), :
        ].astype(jnp.float32)
        for s in range(1, 4):
            total = total + self.got_3[c, s].astype(jnp.float32)
        mine = self.rows(c, self.core, self.q, self.line)
        self.out[mine, :] = total.astype(jnp.bfloat16)
        for s in range(1, 4):
            self.give(self.out.at[mine], self.line_send.at[1, c, s], self.line_recv.at[1, c, s],
                      self.in_line(s)[1])

    def step_5(self, c):
        for s in range(1, 4):
            at, peer = self.in_line(4 - s)
            self.taken(self.out.at[self.rows(c, self.core, self.q, at)],
                       self.line_send.at[1, c, s], self.line_recv.at[1, c, s], peer)
        for s in range(1, self.plane):
            self.give(self.out.at[self.rows(c, self.core, self.q)], self.plane_send.at[1, c, s],
                      self.plane_recv.at[1, c, s], self.in_plane(s)[1])

    def step_6(self, c):
        for s in range(1, self.plane):
            at, peer = self.in_plane(self.plane - s)
            self.taken(self.out.at[self.rows(c, self.core, at)],
                       self.plane_send.at[1, c, s], self.plane_recv.at[1, c, s], peer)
        self.give(self.out.at[self.rows(c, self.core)], self.core_send.at[1, c],
                  self.core_recv.at[1, c], self.mate)

    def step_7(self, c):
        self.taken(self.out.at[self.rows(c, 1 - self.core)], self.core_send.at[1, c],
                   self.core_recv.at[1, c], self.mate)

    def close(self):
        for made in self.sent:
            made.wait_send()


def greet(nodes, groups):
    me, dp = lax.axis_index("space"), lax.axis_index("dp")
    width, core = nodes // 4, lax.rem(dp, 2)
    peers = [(dp, lax.rem(me + step, nodes)) for step in range(1, nodes)]
    peers.append((dp + 1 - 2 * core, me))
    for step in range(1, groups // 2):
        other = lax.rem(dp // 2 + step, groups // 2) * 2 + core
        for w in range(width):
            peers.append((other, (me // width) * width + w))
    barrier = pltpu.get_barrier_semaphore()
    for peer in peers:
        pl.semaphore_signal(barrier, inc=1, device_id=peer, device_id_type=MESH)
    pl.semaphore_wait(barrier, len(peers))


GROUP = 4


def level_kernel(
    nodes, groups, fine, w_fine_in, w_down_in, depth_w_in, gain_in, point_w_in, up_in,
    out, summed,
    w_fine, w_down, depth_w, gain_ref, point_w, up, sem_in,
    f_pad, stack, pre, act, blocks, g_blocks, g_pre_t,
    coarse, c_pad, g_pad, g_own, g_coarse, c_grid, g_grid, depth_out, g_act, small,
    own_1, own_2, slots_1, slots_2, flat,
    got_1, got_2, got_3, part_1, part_2,
    sem_i, sem_j, sem_a, sem_b, sem_c, sem_d, sem_e, sem_f, sem_g, sem_h,
    *sum_sems,
):
    f32, bf16 = jnp.float32, jnp.bfloat16
    fine_x, fine_y, fine_z, chan = fine.shape
    ext_x, ext_y, ext_z, chans = coarse.shape
    cells = ext_x * ext_y * ext_z
    count = nodes * cells
    f_pad[...] = jnp.zeros_like(f_pad)
    c_pad[...] = jnp.zeros_like(c_pad)
    loads = [
        pltpu.make_async_copy(source, dest, sem_in.at[k])
        for k, (source, dest) in enumerate((
            (fine, f_pad.at[pl.ds(1, fine_x), pl.ds(1, fine_y)]),
            (w_fine_in, w_fine), (w_down_in, w_down), (depth_w_in, depth_w),
            (gain_in, gain_ref), (point_w_in, point_w), (up_in, up),
        ))
    ]
    for load in loads:
        load.start()
    g_pad[...] = jnp.zeros_like(g_pad)
    greet(nodes, groups)
    total_of = Summing(nodes, groups, flat, summed, (got_1, got_2, got_3, part_1, part_2), sum_sems)
    halo = halo_copies(fine, f_pad, sem_i, sem_j, nodes)
    start_all(halo)

    def stack_planes(planes):
        spot = lax.broadcasted_iota(jnp.int32, (fine_z, chan), 0)

        def stack_row(y, carry):
            for p in planes:
                row = f_pad[p, y]
                wide = row.astype(f32)
                before = jnp.where(spot == 0, 0.0, pltpu.roll(wide, 1, 0))
                after = jnp.where(spot == fine_z - 1, 0.0, pltpu.roll(wide, fine_z - 1, 0))
                stack[p, y, :, pl.ds(0, chan)] = before.astype(bf16)
                stack[p, y, :, pl.ds(chan, chan)] = row
                stack[p, y, :, pl.ds(2 * chan, chan)] = after.astype(bf16)
            return carry

        lax.fori_loop(0, fine_y + 2, stack_row, 0)

    def conv_planes(planes, first):
        size = GROUP * fine_z

        def conv_group(y_group, carry):
            for x in range(fine_x):
                total = None
                for a in range(3):
                    if x + a not in planes:
                        continue
                    for b in range(3):
                        rows = stack[x + a, pl.ds(y_group * GROUP + b, GROUP)].reshape(size, 3 * chan)
                        term = jnp.dot(
                            rows,
                            w_fine[pl.ds((3 * a + b) * 3 * chan, 3 * chan), :],
                            preferred_element_type=f32,
                        )
                        total = term if total is None else total + term
                at = pl.ds(pl.multiple_of(x * fine_y * fine_z + y_group * size, size), size)
                if total is not None:
                    pre[at, :] = total if first else pre[at, :] + total
            return carry

        lax.fori_loop(0, fine_y // GROUP, conv_group, 0)

    inner, outer = list(range(1, fine_x + 1)), [0, fine_x + 1]
    for load in loads:
        load.wait()
    finish(halo, BESIDE)
    stack_planes(inner)
    conv_planes(inner, True)
    finish(halo, BEYOND)
    stack_planes(outer)
    conv_planes(outer, False)

    def fine_rows(x, y):
        return (x * fine_y + y) * fine_z

    def activate(y, carry):
        for x in range(fine_x):
            at = pl.ds(pl.multiple_of(fine_rows(x, 2 * y), 2 * fine_z), 2 * fine_z)
            value = pre[at, :]
            act[at, :] = (value * jax.nn.sigmoid(value)).astype(bf16).astype(f32)
            for j in range(2):
                for k in range(2):
                    off = 4 * (x % 2) + 2 * j + k
                    part = act[pl.ds(fine_rows(x, 2 * y + j) + k, ext_z, stride=2), :]
                    rows = pl.ds(pl.multiple_of((x // 2 * ext_y + y) * ext_z, ext_z), ext_z)
                    blocks[rows, pl.ds(off * chan, chan)] = part.astype(bf16)
        return carry

    lax.fori_loop(0, ext_y, activate, 0)
    coarse[...] = (
        jnp.dot(blocks[...], w_down[...], preferred_element_type=f32)
        .astype(bf16)
        .reshape(coarse.shape)
    )
    first = halo_copies(coarse, c_pad, sem_a, sem_b, nodes)
    start_all(first)
    c_pad[pl.ds(1, ext_x), pl.ds(1, ext_y)] = coarse[...]
    up_rows = up[...].reshape(cells, chans)
    g_act[...] = lax.dot_general(
        up_rows, point_w[...], (((1,), (1,)), ((), ())), preferred_element_type=f32
    )

    def conv_row(grid, x, y, flip, planes):
        total = None
        for t in range(27):
            a, b, c = tap_offsets(t)
            if x + a not in planes:
                continue
            w_at = 26 - t if flip else t
            term = grid[x + a, y + b, pl.ds(7 + c, ext_z), :] * depth_w[pl.ds(w_at, 1), :]
            total = term if total is None else total + term
        return total

    def cell_rows(x, y):
        return pl.ds(pl.multiple_of((x * ext_y + y) * ext_z, ext_z), ext_z)

    middle, ends = list(range(1, ext_x + 1)), [0, ext_x + 1]
    finish(first, BESIDE)
    for p in middle:
        fill_grid(c_grid, c_pad, p)

    def forward_own(y, carry):
        for x in range(ext_x):
            depth_out[cell_rows(x, y), :] = conv_row(c_grid, x, y, False, middle)
        return carry

    lax.fori_loop(0, ext_y, forward_own, 0)

    def slopes(y, carry):
        for x in range(fine_x):
            at = pl.ds(pl.multiple_of(fine_rows(x, 2 * y), 2 * fine_z), 2 * fine_z)
            value = pre[at, :]
            sigma = jax.nn.sigmoid(value)
            pre[at, :] = sigma * (1.0 + value * (1.0 - sigma))
        return carry

    lax.fori_loop(0, ext_y, slopes, 0)
    finish(first, BEYOND)
    for p in ends:
        fill_grid(c_grid, c_pad, p)

    def forward(y, acc):
        for x in range(ext_x):
            row = depth_out[cell_rows(x, y), :]
            rest = conv_row(c_grid, x, y, False, ends)
            row = row if rest is None else row + rest
            depth_out[cell_rows(x, y), :] = row
            acc = acc + fold8(row * row)
        return acc

    own_1[...] = lax.fori_loop(0, ext_y, forward, jnp.zeros((8, chans), f32))
    spread_1 = spread_copies(own_1, slots_1, sem_c, sem_d, nodes)
    for copy in spread_1:
        copy.start()
    for copy in spread_1:
        copy.wait()
    total = own_1[...]
    for step in range(1, nodes):
        total = total + slots_1[step]
    square_sum = jnp.sum(total, axis=0, keepdims=True)
    gain = gain_ref[...]
    scale = lax.rsqrt(square_sum / count + eps)
    depth_all = depth_out[...]
    normed = (depth_all * (gain * scale)).astype(bf16).astype(f32)
    sigma = jax.nn.sigmoid(normed)
    activated = (normed * sigma).astype(bf16)
    slope = sigma * (1.0 + normed * (1.0 - sigma))
    g_normed = (g_act[...] * slope).astype(bf16).astype(f32)
    g_act[...] = g_normed
    own_2[...] = fold8(g_normed * depth_all)
    spread_2 = spread_copies(own_2, slots_2, sem_e, sem_f, nodes)
    for copy in spread_2:
        copy.start()
    mixed = coarse[...].reshape(cells, chans).astype(f32) + jnp.dot(
        activated, point_w[...], preferred_element_type=f32
    )
    out[...] = mixed.astype(bf16).reshape(coarse.shape)
    down_rows, point_rows = 8 * chan, chans
    at_point, at_small = 2 * down_rows, 2 * down_rows + 2 * point_rows
    at_fine = at_small + 64
    in_point = lax.dot_general(
        activated, up_rows, (((0,), (0,)), ((), ())), preferred_element_type=f32
    ).astype(bf16)
    flat[pl.ds(at_point, point_rows), :] = in_point[:, :LANE]
    flat[pl.ds(at_point + point_rows, point_rows), :] = in_point[:, LANE:]
    small[...] = jnp.zeros_like(small)
    small[pl.ds(27, 1), :] = scale * jnp.sum(own_2[...], axis=0, keepdims=True)
    for copy in spread_2:
        copy.wait()
    total = own_2[...]
    for step in range(1, nodes):
        total = total + slots_2[step]
    cross = jnp.sum(total, axis=0, keepdims=True)
    g_in = gain * scale * g_act[...] - depth_out[...] * (
        gain * scale * scale * scale / count
    ) * cross
    g_own[...] = g_in.astype(bf16).reshape(coarse.shape)
    second = halo_copies(g_own, g_pad, sem_g, sem_h, nodes)
    start_all(second)
    g_pad[pl.ds(1, ext_x), pl.ds(1, ext_y)] = g_own[...]
    for a in range(3):
        def taps(y, acc):
            for x in range(ext_x):
                g_row = g_own[x, y].astype(f32)
                acc = tuple(
                    acc[3 * b + c] + fold8(c_grid[x + a, y + b, pl.ds(7 + c, ext_z), :] * g_row)
                    for b in range(3)
                    for c in range(3)
                )
            return acc
        sums = tuple(jnp.zeros((8, chans), f32) for _ in range(9))
        sums = lax.fori_loop(0, ext_y, taps, sums)
        for k in range(9):
            small[pl.ds(9 * a + k, 1), :] = jnp.sum(sums[k], axis=0, keepdims=True)
    small_16 = small[...].astype(bf16)
    flat[pl.ds(at_small, 32), :] = small_16[:, :LANE]
    flat[pl.ds(at_small + 32, 32), :] = small_16[:, LANE:]
    finish(second, BESIDE + BEYOND)
    for p in middle + ends:
        fill_grid(g_grid, g_pad, p)

    def backward(y, carry):
        for x in range(ext_x):
            row = conv_row(g_grid, x, y, True, middle + ends).astype(bf16).astype(f32)
            g_coarse[cell_rows(x, y), :] = (up[x, y].astype(f32) + row).astype(bf16)
        return carry

    lax.fori_loop(0, ext_y, backward, 0)
    in_down = lax.dot_general(
        blocks[...], g_coarse[...], (((0,), (0,)), ((), ())), preferred_element_type=f32
    ).astype(bf16)
    flat[pl.ds(0, down_rows), :] = in_down[:, :LANE]
    flat[pl.ds(down_rows, down_rows), :] = in_down[:, LANE:]
    total_of.step_1(0)
    g_blocks[...] = lax.dot_general(
        g_coarse[...], w_down[...], (((1,), (1,)), ((), ())), preferred_element_type=f32
    )

    def spread_back(y, carry):
        for x in range(fine_x):
            for j in range(2):
                for k in range(2):
                    off = 4 * (x % 2) + 2 * j + k
                    part = g_blocks[cell_rows(x // 2, y), pl.ds(off * chan, chan)]
                    act[pl.ds(fine_rows(x, 2 * y + j) + k, ext_z, stride=2), :] = part
            start = pl.multiple_of(fine_rows(x, 2 * y), 2 * fine_z)
            at = pl.ds(start, 2 * fine_z)
            g_pre_t[:, at] = (act[at, :] * pre[at, :]).T.astype(bf16)
        return carry

    lax.fori_loop(0, ext_y, spread_back, 0)

    def weight_grads(low, high):
        def one(at, carry):
            rows = stack[pl.ds(at // 3, fine_x), pl.ds(lax.rem(at, 3), fine_y)]
            turned = jnp.dot(
                g_pre_t[...],
                rows.reshape(fine_x * fine_y * fine_z, 3 * chan),
                preferred_element_type=f32,
            )
            for c in range(3):
                start = pl.multiple_of(at_fine + (3 * at + c) * chan, 16)
                flat[pl.ds(start, chan), :] = turned[:, c * chan : (c + 1) * chan].T.astype(bf16)
            return carry

        lax.fori_loop(low, high, one, 0)

    used = at_fine + 27 * chan
    if used < flat.shape[0]:
        flat[pl.ds(used, flat.shape[0] - used), :] = jnp.zeros(
            (flat.shape[0] - used, LANE), bf16
        )
    split = min(9, -(-(2 * (flat.shape[0] // CHUNKS) - at_fine) // (3 * chan)))
    weight_grads(0, split)
    total_of.step_1(1)
    total_of.step_2(0)
    weight_grads(split, 9)
    total_of.step_1(2)
    for c in range(1, CHUNKS):
        total_of.step_2(c)
        total_of.step_3(c - 1)
    total_of.step_4(0)
    total_of.step_3(CHUNKS - 1)
    total_of.step_5(0)
    for c in range(1, CHUNKS):
        total_of.step_4(c)
    for c in range(1, CHUNKS):
        total_of.step_5(c)
    for c in range(CHUNKS):
        total_of.step_6(c)
    for c in range(CHUNKS):
        total_of.step_7(c)
    total_of.close()


def unpack_kernel(
    summed, coarse_in, out, out_fine, out_down, out_depth, out_gain, out_point,
    fine, down, depth, gain, point, sems,
):
    f32 = jnp.float32
    down_rows, point_rows = down.shape[0], point.shape[0]
    at_point, at_small = 2 * down_rows, 2 * down_rows + 2 * point_rows
    at_fine = at_small + 64
    sent = []

    def send(source, dest):
        copy = pltpu.make_async_copy(source, dest, sems.at[len(sent)])
        copy.start()
        sent.append(copy)

    send(coarse_in, out)
    fine[...] = summed[pl.ds(at_fine, fine.shape[0]), :].astype(f32)
    send(fine, out_fine)
    for part in range(2):
        lanes = pl.ds(part * LANE, LANE)
        down[:, lanes] = summed[pl.ds(part * down_rows, down_rows), :].astype(f32)
    send(down, out_down)
    for part in range(2):
        lanes = pl.ds(part * LANE, LANE)
        point[:, lanes] = summed[
            pl.ds(at_point + part * point_rows, point_rows), :
        ].astype(f32)
        small = summed[pl.ds(at_small + 32 * part, 32), :].astype(f32)
        depth[:, lanes] = small[:27]
        gain[:, lanes] = small[27:28]
    send(point, out_point)
    send(depth, out_depth)
    send(gain, out_gain)
    for copy in sent:
        copy.wait()


def whole_level(fine, w_fine, w_down, depth_w, gain, point_w, up, nodes, groups):
    f32, bf16, dma = jnp.float32, jnp.bfloat16, pltpu.SemaphoreType.DMA
    fine_x, fine_y, fine_z, chan = fine.shape
    ext_x, ext_y, ext_z, chans = up.shape
    cells, fine_cells = ext_x * ext_y * ext_z, fine_x * fine_y * fine_z
    padded = (ext_x + 2, ext_y + 2, ext_z, chans)
    grid = (ext_x + 2, ext_y + 2, ext_z + 16, chans)
    plane = groups // 2 * (nodes // 4)
    unit = CHUNKS * 2 * plane * 4 * 16
    rows = 16 * chan + 2 * chans + 64 + 27 * chan
    rows = -(-rows // unit) * unit
    piece = rows // (CHUNKS * 2 * plane * 4)
    results = (
            jax.ShapeDtypeStruct(up.shape, bf16),
            jax.ShapeDtypeStruct((27 * chan, chan), f32),
            jax.ShapeDtypeStruct((8 * chan, chans), f32),
            jax.ShapeDtypeStruct((27, chans), f32),
            jax.ShapeDtypeStruct((1, chans), f32),
            jax.ShapeDtypeStruct((chans, chans), f32),
    )
    coarse_out, summed = pl.pallas_call(
        functools.partial(level_kernel, nodes, groups),
        out_shape=(
            jax.ShapeDtypeStruct(up.shape, bf16),
            jax.ShapeDtypeStruct((rows, LANE), bf16),
        ),
        in_specs=[ANY_SPEC] * 7,
        out_specs=(VMEM_SPEC,) * 2,
        scratch_shapes=[
            pltpu.VMEM((27 * chan, chan), bf16),
            pltpu.VMEM(w_down.shape, bf16),
            pltpu.VMEM(depth_w.shape, f32),
            pltpu.VMEM((1, chans), f32),
            pltpu.VMEM(point_w.shape, bf16),
            pltpu.VMEM(up.shape, bf16),
            dma((7,)),
            pltpu.VMEM((fine_x + 2, fine_y + 2, fine_z, chan), bf16),
            pltpu.VMEM((fine_x + 2, fine_y + 2, fine_z, 3 * chan), bf16),
            pltpu.VMEM((fine_cells, chan), f32),
            pltpu.VMEM((fine_cells, chan), f32),
            pltpu.VMEM((cells, 8 * chan), bf16),
            pltpu.VMEM((cells, 8 * chan), f32),
            pltpu.VMEM((chan, fine_cells), bf16),
            pltpu.VMEM(up.shape, bf16),
            pltpu.VMEM(padded, bf16),
            pltpu.VMEM(padded, bf16),
            pltpu.VMEM(up.shape, bf16),
            pltpu.VMEM((cells, chans), bf16),
            pltpu.VMEM(grid, f32),
            pltpu.VMEM(grid, f32),
            pltpu.VMEM((cells, chans), f32),
            pltpu.VMEM((cells, chans), f32),
            pltpu.VMEM((32, chans), f32),
            pltpu.VMEM((8, chans), f32),
            pltpu.VMEM((8, chans), f32),
            pltpu.VMEM((nodes, 8, chans), f32),
            pltpu.VMEM((nodes, 8, chans), f32),
            pltpu.VMEM((rows, LANE), bf16),
            pltpu.VMEM((CHUNKS, plane * 4 * piece, LANE), bf16),
            pltpu.VMEM((CHUNKS, plane, 4 * piece, LANE), bf16),
            pltpu.VMEM((CHUNKS, 4, piece, LANE), bf16),
            pltpu.VMEM((CHUNKS, plane * 4 * piece, LANE), bf16),
            pltpu.VMEM((CHUNKS, 4 * piece, LANE), bf16),
            dma((8,)), dma((8,)),
            dma((8,)), dma((8,)), dma((nodes,)), dma((nodes,)),
            dma((nodes,)), dma((nodes,)), dma((8,)), dma((8,)),
            dma((2, CHUNKS)), dma((2, CHUNKS)),
            dma((2, CHUNKS, plane)), dma((2, CHUNKS, plane)),
            dma((2, CHUNKS, 4)), dma((2, CHUNKS, 4)),
        ],
        compiler_params=pltpu.CompilerParams(
            collective_id=0, has_side_effects=True, vmem_limit_bytes=VMEM_BYTES
        ),
        name="whole_level",
    )(fine, w_fine.reshape(-1, w_fine.shape[2]), w_down, depth_w, gain.reshape(1, chans), point_w, up)
    return pl.pallas_call(
        unpack_kernel,
        out_shape=results,
        in_specs=[VMEM_SPEC] * 2,
        out_specs=(ANY_SPEC,) * 6,
        scratch_shapes=[pltpu.VMEM(one.shape, one.dtype) for one in results[1:]] + [dma((6,))],
        compiler_params=pltpu.CompilerParams(vmem_limit_bytes=VMEM_BYTES),
        name="unpack",
    )(summed, coarse_out)


def local(fields, conv_fine, conv_down, conv_depth, norm_gain, conv_point, upstream):
    nodes, groups = lax.axis_size("space"), lax.axis_size("dp")
    coarse_out, fine, down, depth, gain, point = whole_level(
        fields[0, 0], conv_fine, conv_down, conv_depth, norm_gain, conv_point, upstream[0, 0],
        nodes, groups,
    )
    return (
        coarse_out[None, None], fine.reshape(conv_fine.shape), down, depth, gain.reshape(-1), point
    )


def solution(mesh):
    placed = (
        P("dp", "space", None, None, None, None),
        P(),
        P(),
        P(),
        P(),
        P(),
        P("dp", "space", None, None, None, None),
    )
    return jax.shard_map(
        local,
        mesh=mesh,
        in_specs=placed,
        out_specs=(P("dp", "space", None, None, None, None), P(), P(), P(), P(), P()),
        check_vma=False,
    )
```

```python
import functools
import jax
import jax.numpy as jnp
from jax import lax
from jax.experimental import pallas as pl
from jax.experimental.pallas import tpu as pltpu
from jax.sharding import PartitionSpec as P

eps = 1e-05
MESH = pl.DeviceIdType.MESH
OFFSETS = [(dx, dy) for dx in (-1, 0, 1) for dy in (-1, 0, 1) if (dx, dy) != (0, 0)]
VMEM_SPEC = pl.BlockSpec(memory_space=pltpu.VMEM)
ANY_SPEC = pl.BlockSpec(memory_space=pl.ANY)
VMEM_BYTES = 61 * 1024 * 1024


def tap_offsets(tap_index):
    return (tap_index // 9, tap_index // 3 % 3, tap_index % 3)


def edge_of(delta, ext):
    return {-1: pl.ds(0, 1), 0: pl.ds(0, ext), 1: pl.ds(ext - 1, 1)}[delta]


def rim_of(delta, ext):
    return {-1: pl.ds(0, 1), 0: pl.ds(1, ext), 1: pl.ds(ext + 1, 1)}[delta]


def halo_copies(src, dst, send_sem, recv_sem, nodes):
    me, dp = lax.axis_index("space"), lax.axis_index("dp")
    ext_x, ext_y = src.shape[0], src.shape[1]
    pos_x, pos_y = me // 4, lax.rem(me, 4)
    result = []
    for k, (dx, dy) in enumerate(OFFSETS):
        exists = jnp.logical_and(
            jnp.logical_and(pos_x + dx >= 0, pos_x + dx < nodes // 4),
            jnp.logical_and(pos_y + dy >= 0, pos_y + dy < 4),
        )
        source = src.at[edge_of(dx, ext_x), edge_of(dy, ext_y)]
        peer = (dp, me + 4 * dx + dy)
        send = pltpu.make_async_remote_copy(
            src_ref=source,
            dst_ref=dst.at[rim_of(-dx, ext_x), rim_of(-dy, ext_y)],
            send_sem=send_sem.at[k],
            recv_sem=recv_sem.at[7 - k],
            device_id=peer,
            device_id_type=MESH,
        )
        arrival = pltpu.make_async_remote_copy(
            src_ref=source,
            dst_ref=dst.at[rim_of(dx, ext_x), rim_of(dy, ext_y)],
            send_sem=send_sem.at[k],
            recv_sem=recv_sem.at[k],
            device_id=peer,
            device_id_type=MESH,
        )
        result.append((exists, send, arrival))
    return result


def start_all(copies):
    for k in (3, 4, 1, 6, 0, 2, 5, 7):
        exists, send, _ = copies[k]
        pl.when(exists)(send.start)


def finish(copies, which):
    for k in which:
        exists, _, arrival = copies[k]
        pl.when(exists)(arrival.wait)


BESIDE, BEYOND = (3, 4), (0, 1, 2, 5, 6, 7)


def fold8(rows):
    return jnp.sum(rows.reshape(rows.shape[0] // 8, 8, rows.shape[1]), axis=0)


def spread_copies(own, slots, send_sem, recv_sem, nodes):
    me, dp = lax.axis_index("space"), lax.axis_index("dp")
    return [
        pltpu.make_async_remote_copy(
            src_ref=own,
            dst_ref=slots.at[step],
            send_sem=send_sem.at[step],
            recv_sem=recv_sem.at[step],
            device_id=(dp, lax.rem(me + step, nodes)),
            device_id_type=MESH,
        )
        for step in range(1, nodes)
    ]


def fill_grid(grid, padded, plane):
    ext_z = padded.shape[2]
    side = jnp.zeros((grid.shape[1], 8, grid.shape[3]), jnp.float32)
    grid[plane, :, pl.ds(0, 8)] = side
    grid[plane, :, pl.ds(8 + ext_z, 8)] = side
    grid[plane, :, pl.ds(8, ext_z)] = padded[plane].astype(jnp.float32)


CHUNKS = 3
LANE = 128


class Summing:
    def __init__(self, nodes, groups, src, out, bufs, sems):
        self.src, self.out = src, out
        self.got_1, self.got_2, self.got_3, self.part_1, self.part_2 = bufs
        self.core_send, self.core_recv, self.plane_send, self.plane_recv, self.line_send, self.line_recv = sems
        self.width = nodes // 4
        self.plane = groups // 2 * self.width
        self.me, self.dp = lax.axis_index("space"), lax.axis_index("dp")
        self.core = lax.rem(self.dp, 2)
        self.line = self.me // self.width
        self.q = (self.dp // 2) * self.width + lax.rem(self.me, self.width)
        self.mate = (self.dp + 1 - 2 * self.core, self.me)
        self.piece = src.shape[0] // (CHUNKS * 2 * self.plane * 4)
        self.made, self.sent = {}, []

    def in_plane(self, step):
        at = lax.rem(self.q + step, self.plane)
        return at, (
            (at // self.width) * 2 + self.core,
            self.line * self.width + lax.rem(at, self.width),
        )

    def in_line(self, step):
        at = lax.rem(self.line + step, 4)
        return at, (self.dp, at * self.width + lax.rem(self.me, self.width))

    def rows(self, c, h, q=None, line=None):
        count = self.piece
        at = (c * 2 + h) * self.plane
        if q is None:
            at, count = at * 4, count * self.plane * 4
        elif line is None:
            at, count = (at + q) * 4, count * 4
        else:
            at = (at + q) * 4 + line
        return pl.ds(pl.multiple_of(at * self.piece, 16), count)

    def copy(self, source, dest, send_sem, recv_sem, peer):
        return pltpu.make_async_remote_copy(
            src_ref=source, dst_ref=dest, send_sem=send_sem, recv_sem=recv_sem,
            device_id=peer, device_id_type=MESH,
        )

    def push(self, key, *args):
        made = self.copy(*args)
        made.start()
        self.made.setdefault(key, []).append(made)

    def give(self, dest, *args):
        made = self.copy(dest, dest, *args)
        made.start()
        self.sent.append(made)

    def taken(self, dest, *args):
        self.copy(dest, dest, *args).wait_recv()

    def finished(self, key):
        for made in self.made[key]:
            made.wait()

    def step_1(self, c):
        self.push((1, c), self.src.at[self.rows(c, 1 - self.core)], self.got_1.at[c],
                  self.core_send.at[0, c], self.core_recv.at[0, c], self.mate)

    def step_2(self, c):
        self.finished((1, c))
        own = self.src[self.rows(c, self.core), :].astype(jnp.float32)
        self.part_1[c] = (own + self.got_1[c].astype(jnp.float32)).astype(jnp.bfloat16)
        count = 4 * self.piece
        for s in range(1, self.plane):
            at, peer = self.in_plane(s)
            self.push((2, c), self.part_1.at[c, pl.ds(pl.multiple_of(at * count, 16), count)],
                      self.got_2.at[c, s], self.plane_send.at[0, c, s],
                      self.plane_recv.at[0, c, s], peer)

    def step_3(self, c):
        self.finished((2, c))
        count = 4 * self.piece
        total = self.part_1[c, pl.ds(pl.multiple_of(self.q * count, 16), count), :].astype(jnp.float32)
        for s in range(1, self.plane):
            total = total + self.got_2[c, s].astype(jnp.float32)
        self.part_2[c] = total.astype(jnp.bfloat16)
        for s in range(1, 4):
            at, peer = self.in_line(s)
            self.push((3, c),
                      self.part_2.at[c, pl.ds(pl.multiple_of(at * self.piece, 16), self.piece)],
                      self.got_3.at[c, s], self.line_send.at[0, c, s],
                      self.line_recv.at[0, c, s], peer)

    def step_4(self, c):
        self.finished((3, c))
        total = self.part_2[
            c, pl.ds(pl.multiple_of(self.line * self.piece, 16), self.piece), :
        ].astype(jnp.float32)
        for s in range(1, 4):
            total = total + self.got_3[c, s].astype(jnp.float32)
        mine = self.rows(c, self.core, self.q, self.line)
        self.out[mine, :] = total.astype(jnp.bfloat16)
        for s in range(1, 4):
            self.give(self.out.at[mine], self.line_send.at[1, c, s], self.line_recv.at[1, c, s],
                      self.in_line(s)[1])

    def step_5(self, c):
        for s in range(1, 4):
            at, peer = self.in_line(4 - s)
            self.taken(self.out.at[self.rows(c, self.core, self.q, at)],
                       self.line_send.at[1, c, s], self.line_recv.at[1, c, s], peer)
        for s in range(1, self.plane):
            self.give(self.out.at[self.rows(c, self.core, self.q)], self.plane_send.at[1, c, s],
                      self.plane_recv.at[1, c, s], self.in_plane(s)[1])

    def step_6(self, c):
        for s in range(1, self.plane):
            at, peer = self.in_plane(self.plane - s)
            self.taken(self.out.at[self.rows(c, self.core, at)],
                       self.plane_send.at[1, c, s], self.plane_recv.at[1, c, s], peer)
        self.give(self.out.at[self.rows(c, self.core)], self.core_send.at[1, c],
                  self.core_recv.at[1, c], self.mate)

    def step_7(self, c):
        self.taken(self.out.at[self.rows(c, 1 - self.core)], self.core_send.at[1, c],
                   self.core_recv.at[1, c], self.mate)

    def close(self):
        for made in self.sent:
            made.wait_send()


def greet(nodes, groups):
    me, dp = lax.axis_index("space"), lax.axis_index("dp")
    width, core = nodes // 4, lax.rem(dp, 2)
    peers = [(dp, lax.rem(me + step, nodes)) for step in range(1, nodes)]
    peers.append((dp + 1 - 2 * core, me))
    for step in range(1, groups // 2):
        other = lax.rem(dp // 2 + step, groups // 2) * 2 + core
        for w in range(width):
            peers.append((other, (me // width) * width + w))
    barrier = pltpu.get_barrier_semaphore()
    for peer in peers:
        pl.semaphore_signal(barrier, inc=1, device_id=peer, device_id_type=MESH)
    pl.semaphore_wait(barrier, len(peers))


GROUP = 4


def level_kernel(
    nodes, groups, fine, w_fine_in, w_down_in, depth_w_in, gain_in, point_w_in, up_in,
    out, summed,
    w_fine, w_down, depth_w, gain_ref, point_w, up, sem_in,
    f_pad, stack, pre, act, blocks, g_blocks, g_pre_t,
    coarse, c_pad, g_pad, g_own, g_coarse, c_grid, g_grid, depth_out, g_act, small,
    own_1, own_2, slots_1, slots_2, flat,
    got_1, got_2, got_3, part_1, part_2,
    sem_i, sem_j, sem_a, sem_b, sem_c, sem_d, sem_e, sem_f, sem_g, sem_h,
    *sum_sems,
):
    f32, bf16 = jnp.float32, jnp.bfloat16
    fine_x, fine_y, fine_z, chan = fine.shape
    ext_x, ext_y, ext_z, chans = coarse.shape
    cells = ext_x * ext_y * ext_z
    count = nodes * cells
    f_pad[...] = jnp.zeros_like(f_pad)
    c_pad[...] = jnp.zeros_like(c_pad)
    loads = [
        pltpu.make_async_copy(source, dest, sem_in.at[k])
        for k, (source, dest) in enumerate((
            (fine, f_pad.at[pl.ds(1, fine_x), pl.ds(1, fine_y)]),
            (w_fine_in, w_fine), (w_down_in, w_down), (depth_w_in, depth_w),
            (gain_in, gain_ref), (point_w_in, point_w), (up_in, up),
        ))
    ]
    for load in loads:
        load.start()
    g_pad[...] = jnp.zeros_like(g_pad)
    greet(nodes, groups)
    total_of = Summing(nodes, groups, flat, summed, (got_1, got_2, got_3, part_1, part_2), sum_sems)
    halo = halo_copies(fine, f_pad, sem_i, sem_j, nodes)
    start_all(halo)

    def stack_planes(planes):
        spot = lax.broadcasted_iota(jnp.int32, (fine_z, chan), 0)

        def stack_row(y, carry):
            for p in planes:
                row = f_pad[p, y]
                wide = row.astype(f32)
                before = jnp.where(spot == 0, 0.0, pltpu.roll(wide, 1, 0))
                after = jnp.where(spot == fine_z - 1, 0.0, pltpu.roll(wide, fine_z - 1, 0))
                stack[p, y, :, pl.ds(0, chan)] = before.astype(bf16)
                stack[p, y, :, pl.ds(chan, chan)] = row
                stack[p, y, :, pl.ds(2 * chan, chan)] = after.astype(bf16)
            return carry

        lax.fori_loop(0, fine_y + 2, stack_row, 0)

    def conv_planes(planes, first):
        size = GROUP * fine_z

        def conv_group(y_group, carry):
            for x in range(fine_x):
                total = None
                for a in range(3):
                    if x + a not in planes:
                        continue
                    for b in range(3):
                        rows = stack[x + a, pl.ds(y_group * GROUP + b, GROUP)].reshape(size, 3 * chan)
                        term = jnp.dot(
                            rows,
                            w_fine[pl.ds((3 * a + b) * 3 * chan, 3 * chan), :],
                            preferred_element_type=f32,
                        )
                        total = term if total is None else total + term
                at = pl.ds(pl.multiple_of(x * fine_y * fine_z + y_group * size, size), size)
                if total is not None:
                    pre[at, :] = total if first else pre[at, :] + total
            return carry

        lax.fori_loop(0, fine_y // GROUP, conv_group, 0)

    inner, outer = list(range(1, fine_x + 1)), [0, fine_x + 1]
    for load in loads:
        load.wait()
    finish(halo, BESIDE)
    stack_planes(inner)
    conv_planes(inner, True)
    finish(halo, BEYOND)
    stack_planes(outer)
    conv_planes(outer, False)

    def fine_rows(x, y):
        return (x * fine_y + y) * fine_z

    def activate(y, carry):
        for x in range(fine_x):
            at = pl.ds(pl.multiple_of(fine_rows(x, 2 * y), 2 * fine_z), 2 * fine_z)
            value = pre[at, :]
            act[at, :] = (value * jax.nn.sigmoid(value)).astype(bf16).astype(f32)
            for j in range(2):
                for k in range(2):
                    off = 4 * (x % 2) + 2 * j + k
                    part = act[pl.ds(fine_rows(x, 2 * y + j) + k, ext_z, stride=2), :]
                    rows = pl.ds(pl.multiple_of((x // 2 * ext_y + y) * ext_z, ext_z), ext_z)
                    blocks[rows, pl.ds(off * chan, chan)] = part.astype(bf16)
        return carry

    lax.fori_loop(0, ext_y, activate, 0)
    coarse[...] = (
        jnp.dot(blocks[...], w_down[...], preferred_element_type=f32)
        .astype(bf16)
        .reshape(coarse.shape)
    )
    first = halo_copies(coarse, c_pad, sem_a, sem_b, nodes)
    start_all(first)
    c_pad[pl.ds(1, ext_x), pl.ds(1, ext_y)] = coarse[...]
    up_rows = up[...].reshape(cells, chans)
    g_act[...] = lax.dot_general(
        up_rows, point_w[...], (((1,), (1,)), ((), ())), preferred_element_type=f32
    )

    def conv_row(grid, x, y, flip, planes):
        total = None
        for t in range(27):
            a, b, c = tap_offsets(t)
            if x + a not in planes:
                continue
            w_at = 26 - t if flip else t
            term = grid[x + a, y + b, pl.ds(7 + c, ext_z), :] * depth_w[pl.ds(w_at, 1), :]
            total = term if total is None else total + term
        return total

    def cell_rows(x, y):
        return pl.ds(pl.multiple_of((x * ext_y + y) * ext_z, ext_z), ext_z)

    middle, ends = list(range(1, ext_x + 1)), [0, ext_x + 1]
    finish(first, BESIDE)
    for p in middle:
        fill_grid(c_grid, c_pad, p)

    def forward_own(y, carry):
        for x in range(ext_x):
            depth_out[cell_rows(x, y), :] = conv_row(c_grid, x, y, False, middle)
        return carry

    lax.fori_loop(0, ext_y, forward_own, 0)

    def slopes(y, carry):
        for x in range(fine_x):
            at = pl.ds(pl.multiple_of(fine_rows(x, 2 * y), 2 * fine_z), 2 * fine_z)
            value = pre[at, :]
            sigma = jax.nn.sigmoid(value)
            pre[at, :] = sigma * (1.0 + value * (1.0 - sigma))
        return carry

    lax.fori_loop(0, ext_y, slopes, 0)
    finish(first, BEYOND)
    for p in ends:
        fill_grid(c_grid, c_pad, p)

    def forward(y, acc):
        for x in range(ext_x):
            row = depth_out[cell_rows(x, y), :]
            rest = conv_row(c_grid, x, y, False, ends)
            row = row if rest is None else row + rest
            depth_out[cell_rows(x, y), :] = row
            acc = acc + fold8(row * row)
        return acc

    own_1[...] = lax.fori_loop(0, ext_y, forward, jnp.zeros((8, chans), f32))
    spread_1 = spread_copies(own_1, slots_1, sem_c, sem_d, nodes)
    for copy in spread_1:
        copy.start()
    for copy in spread_1:
        copy.wait()
    total = own_1[...]
    for step in range(1, nodes):
        total = total + slots_1[step]
    square_sum = jnp.sum(total, axis=0, keepdims=True)
    gain = gain_ref[...]
    scale = lax.rsqrt(square_sum / count + eps)
    depth_all = depth_out[...]
    normed = (depth_all * (gain * scale)).astype(bf16).astype(f32)
    sigma = jax.nn.sigmoid(normed)
    activated = (normed * sigma).astype(bf16)
    slope = sigma * (1.0 + normed * (1.0 - sigma))
    g_normed = (g_act[...] * slope).astype(bf16).astype(f32)
    g_act[...] = g_normed
    own_2[...] = fold8(g_normed * depth_all)
    spread_2 = spread_copies(own_2, slots_2, sem_e, sem_f, nodes)
    for copy in spread_2:
        copy.start()
    mixed = coarse[...].reshape(cells, chans).astype(f32) + jnp.dot(
        activated, point_w[...], preferred_element_type=f32
    )
    out[...] = mixed.astype(bf16).reshape(coarse.shape)
    down_rows, point_rows = 8 * chan, chans
    at_point, at_small = 2 * down_rows, 2 * down_rows + 2 * point_rows
    at_fine = at_small + 64
    in_point = lax.dot_general(
        activated, up_rows, (((0,), (0,)), ((), ())), preferred_element_type=f32
    ).astype(bf16)
    flat[pl.ds(at_point, point_rows), :] = in_point[:, :LANE]
    flat[pl.ds(at_point + point_rows, point_rows), :] = in_point[:, LANE:]
    small[...] = jnp.zeros_like(small)
    small[pl.ds(27, 1), :] = scale * jnp.sum(own_2[...], axis=0, keepdims=True)
    for copy in spread_2:
        copy.wait()
    total = own_2[...]
    for step in range(1, nodes):
        total = total + slots_2[step]
    cross = jnp.sum(total, axis=0, keepdims=True)
    g_in = gain * scale * g_act[...] - depth_out[...] * (
        gain * scale * scale * scale / count
    ) * cross
    g_own[...] = g_in.astype(bf16).reshape(coarse.shape)
    second = halo_copies(g_own, g_pad, sem_g, sem_h, nodes)
    start_all(second)
    g_pad[pl.ds(1, ext_x), pl.ds(1, ext_y)] = g_own[...]
    for a in range(3):
        def taps(y, acc):
            for x in range(ext_x):
                g_row = g_own[x, y].astype(f32)
                acc = tuple(
                    acc[3 * b + c] + fold8(c_grid[x + a, y + b, pl.ds(7 + c, ext_z), :] * g_row)
                    for b in range(3)
                    for c in range(3)
                )
            return acc
        sums = tuple(jnp.zeros((8, chans), f32) for _ in range(9))
        sums = lax.fori_loop(0, ext_y, taps, sums)
        for k in range(9):
            small[pl.ds(9 * a + k, 1), :] = jnp.sum(sums[k], axis=0, keepdims=True)
    small_16 = small[...].astype(bf16)
    flat[pl.ds(at_small, 32), :] = small_16[:, :LANE]
    flat[pl.ds(at_small + 32, 32), :] = small_16[:, LANE:]
    finish(second, BESIDE + BEYOND)
    for p in middle + ends:
        fill_grid(g_grid, g_pad, p)

    def backward(y, carry):
        for x in range(ext_x):
            row = conv_row(g_grid, x, y, True, middle + ends).astype(bf16).astype(f32)
            g_coarse[cell_rows(x, y), :] = (up[x, y].astype(f32) + row).astype(bf16)
        return carry

    lax.fori_loop(0, ext_y, backward, 0)
    in_down = lax.dot_general(
        blocks[...], g_coarse[...], (((0,), (0,)), ((), ())), preferred_element_type=f32
    ).astype(bf16)
    flat[pl.ds(0, down_rows), :] = in_down[:, :LANE]
    flat[pl.ds(down_rows, down_rows), :] = in_down[:, LANE:]
    total_of.step_1(0)
    g_blocks[...] = lax.dot_general(
        g_coarse[...], w_down[...], (((1,), (1,)), ((), ())), preferred_element_type=f32
    )

    def spread_back(y, carry):
        for x in range(fine_x):
            for j in range(2):
                for k in range(2):
                    off = 4 * (x % 2) + 2 * j + k
                    part = g_blocks[cell_rows(x // 2, y), pl.ds(off * chan, chan)]
                    act[pl.ds(fine_rows(x, 2 * y + j) + k, ext_z, stride=2), :] = part
            start = pl.multiple_of(fine_rows(x, 2 * y), 2 * fine_z)
            at = pl.ds(start, 2 * fine_z)
            g_pre_t[:, at] = (act[at, :] * pre[at, :]).T.astype(bf16)
        return carry

    lax.fori_loop(0, ext_y, spread_back, 0)

    def weight_grads(low, high):
        def one(at, carry):
            rows = stack[pl.ds(at // 3, fine_x), pl.ds(lax.rem(at, 3), fine_y)]
            turned = jnp.dot(
                g_pre_t[...],
                rows.reshape(fine_x * fine_y * fine_z, 3 * chan),
                preferred_element_type=f32,
            )
            for c in range(3):
                start = pl.multiple_of(at_fine + (3 * at + c) * chan, 16)
                flat[pl.ds(start, chan), :] = turned[:, c * chan : (c + 1) * chan].T.astype(bf16)
            return carry

        lax.fori_loop(low, high, one, 0)

    used = at_fine + 27 * chan
    if used < flat.shape[0]:
        flat[pl.ds(used, flat.shape[0] - used), :] = jnp.zeros(
            (flat.shape[0] - used, LANE), bf16
        )
    split = min(9, -(-(2 * (flat.shape[0] // CHUNKS) - at_fine) // (3 * chan)))
    half = (split + 9) // 2
    total_of.step_2(0)
    weight_grads(0, split)
    total_of.step_1(1)
    total_of.step_3(0)
    weight_grads(split, half)
    total_of.step_2(1)
    total_of.step_4(0)
    weight_grads(half, 9)
    total_of.step_1(2)
    total_of.step_3(1)
    total_of.step_5(0)
    total_of.step_2(2)
    total_of.step_4(1)
    total_of.step_6(0)
    total_of.step_3(2)
    total_of.step_5(1)
    total_of.step_4(2)
    total_of.step_6(1)
    total_of.step_5(2)
    total_of.step_6(2)
    for c in range(CHUNKS):
        total_of.step_7(c)
    total_of.close()


def unpack_kernel(
    summed, coarse_in, out, out_fine, out_down, out_depth, out_gain, out_point,
    fine, down, depth, gain, point, sems,
):
    f32 = jnp.float32
    down_rows, point_rows = down.shape[0], point.shape[0]
    at_point, at_small = 2 * down_rows, 2 * down_rows + 2 * point_rows
    at_fine = at_small + 64
    sent = []

    def send(source, dest):
        copy = pltpu.make_async_copy(source, dest, sems.at[len(sent)])
        copy.start()
        sent.append(copy)

    send(coarse_in, out)
    fine[...] = summed[pl.ds(at_fine, fine.shape[0]), :].astype(f32)
    send(fine, out_fine)
    for part in range(2):
        lanes = pl.ds(part * LANE, LANE)
        down[:, lanes] = summed[pl.ds(part * down_rows, down_rows), :].astype(f32)
    send(down, out_down)
    for part in range(2):
        lanes = pl.ds(part * LANE, LANE)
        point[:, lanes] = summed[
            pl.ds(at_point + part * point_rows, point_rows), :
        ].astype(f32)
        small = summed[pl.ds(at_small + 32 * part, 32), :].astype(f32)
        depth[:, lanes] = small[:27]
        gain[:, lanes] = small[27:28]
    send(point, out_point)
    send(depth, out_depth)
    send(gain, out_gain)
    for copy in sent:
        copy.wait()


def whole_level(fine, w_fine, w_down, depth_w, gain, point_w, up, nodes, groups):
    f32, bf16, dma = jnp.float32, jnp.bfloat16, pltpu.SemaphoreType.DMA
    fine_x, fine_y, fine_z, chan = fine.shape
    ext_x, ext_y, ext_z, chans = up.shape
    cells, fine_cells = ext_x * ext_y * ext_z, fine_x * fine_y * fine_z
    padded = (ext_x + 2, ext_y + 2, ext_z, chans)
    grid = (ext_x + 2, ext_y + 2, ext_z + 16, chans)
    plane = groups // 2 * (nodes // 4)
    unit = CHUNKS * 2 * plane * 4 * 16
    rows = 16 * chan + 2 * chans + 64 + 27 * chan
    rows = -(-rows // unit) * unit
    piece = rows // (CHUNKS * 2 * plane * 4)
    results = (
            jax.ShapeDtypeStruct(up.shape, bf16),
            jax.ShapeDtypeStruct((27 * chan, chan), f32),
            jax.ShapeDtypeStruct((8 * chan, chans), f32),
            jax.ShapeDtypeStruct((27, chans), f32),
            jax.ShapeDtypeStruct((1, chans), f32),
            jax.ShapeDtypeStruct((chans, chans), f32),
    )
    coarse_out, summed = pl.pallas_call(
        functools.partial(level_kernel, nodes, groups),
        out_shape=(
            jax.ShapeDtypeStruct(up.shape, bf16),
            jax.ShapeDtypeStruct((rows, LANE), bf16),
        ),
        in_specs=[ANY_SPEC] * 7,
        out_specs=(VMEM_SPEC,) * 2,
        scratch_shapes=[
            pltpu.VMEM((27 * chan, chan), bf16),
            pltpu.VMEM(w_down.shape, bf16),
            pltpu.VMEM(depth_w.shape, f32),
            pltpu.VMEM((1, chans), f32),
            pltpu.VMEM(point_w.shape, bf16),
            pltpu.VMEM(up.shape, bf16),
            dma((7,)),
            pltpu.VMEM((fine_x + 2, fine_y + 2, fine_z, chan), bf16),
            pltpu.VMEM((fine_x + 2, fine_y + 2, fine_z, 3 * chan), bf16),
            pltpu.VMEM((fine_cells, chan), f32),
            pltpu.VMEM((fine_cells, chan), f32),
            pltpu.VMEM((cells, 8 * chan), bf16),
            pltpu.VMEM((cells, 8 * chan), f32),
            pltpu.VMEM((chan, fine_cells), bf16),
            pltpu.VMEM(up.shape, bf16),
            pltpu.VMEM(padded, bf16),
            pltpu.VMEM(padded, bf16),
            pltpu.VMEM(up.shape, bf16),
            pltpu.VMEM((cells, chans), bf16),
            pltpu.VMEM(grid, f32),
            pltpu.VMEM(grid, f32),
            pltpu.VMEM((cells, chans), f32),
            pltpu.VMEM((cells, chans), f32),
            pltpu.VMEM((32, chans), f32),
            pltpu.VMEM((8, chans), f32),
            pltpu.VMEM((8, chans), f32),
            pltpu.VMEM((nodes, 8, chans), f32),
            pltpu.VMEM((nodes, 8, chans), f32),
            pltpu.VMEM((rows, LANE), bf16),
            pltpu.VMEM((CHUNKS, plane * 4 * piece, LANE), bf16),
            pltpu.VMEM((CHUNKS, plane, 4 * piece, LANE), bf16),
            pltpu.VMEM((CHUNKS, 4, piece, LANE), bf16),
            pltpu.VMEM((CHUNKS, plane * 4 * piece, LANE), bf16),
            pltpu.VMEM((CHUNKS, 4 * piece, LANE), bf16),
            dma((8,)), dma((8,)),
            dma((8,)), dma((8,)), dma((nodes,)), dma((nodes,)),
            dma((nodes,)), dma((nodes,)), dma((8,)), dma((8,)),
            dma((2, CHUNKS)), dma((2, CHUNKS)),
            dma((2, CHUNKS, plane)), dma((2, CHUNKS, plane)),
            dma((2, CHUNKS, 4)), dma((2, CHUNKS, 4)),
        ],
        compiler_params=pltpu.CompilerParams(
            collective_id=0, has_side_effects=True, vmem_limit_bytes=VMEM_BYTES
        ),
        name="whole_level",
    )(fine, w_fine.reshape(-1, w_fine.shape[2]), w_down, depth_w, gain.reshape(1, chans), point_w, up)
    return pl.pallas_call(
        unpack_kernel,
        out_shape=results,
        in_specs=[VMEM_SPEC] * 2,
        out_specs=(ANY_SPEC,) * 6,
        scratch_shapes=[pltpu.VMEM(one.shape, one.dtype) for one in results[1:]] + [dma((6,))],
        compiler_params=pltpu.CompilerParams(vmem_limit_bytes=VMEM_BYTES),
        name="unpack",
    )(summed, coarse_out)


def local(fields, conv_fine, conv_down, conv_depth, norm_gain, conv_point, upstream):
    nodes, groups = lax.axis_size("space"), lax.axis_size("dp")
    coarse_out, fine, down, depth, gain, point = whole_level(
        fields[0, 0], conv_fine, conv_down, conv_depth, norm_gain, conv_point, upstream[0, 0],
        nodes, groups,
    )
    return (
        coarse_out[None, None], fine.reshape(conv_fine.shape), down, depth, gain.reshape(-1), point
    )


def solution(mesh):
    placed = (
        P("dp", "space", None, None, None, None),
        P(),
        P(),
        P(),
        P(),
        P(),
        P("dp", "space", None, None, None, None),
    )
    return jax.shard_map(
        local,
        mesh=mesh,
        in_specs=placed,
        out_specs=(P("dp", "space", None, None, None, None), P(), P(), P(), P(), P()),
        check_vma=False,
    )
```
